32 devices in a mesh: wind: 2 (over y), gx: 4 (over z), gy: 2 (over x), gz: 2 (over core).
Axes of the slice: x: 2, y: 2, z: 4, core: 2. Of those that a mesh axis runs over, the one named last changes fastest.
Arguments:
- pressure: bfloat16 [8192, 8192], P(('wind', 'gx'), ('gy', 'gz')), parts along dimension 0, may hold values from -40 to 40
- fir_taps: bfloat16 [257], replicated, may hold values from -0.375 to 0.375
- influence: bfloat16 [256, 4, 4, 512], P(None, ('gy', 'gz'), 'gx'), may hold values from -0.0625 to 0.0625
- mode_impulse: float32 [256, 64], replicated, may hold values from -0.75 to 0.75
- mode_taps: int32 [256], replicated, may hold values from 1 to 64, as said below
Outputs:
- responses: bfloat16 [512, 4096], P(('wind', 'gx', 'gy', 'gz')), parts along dimension 0
- correlation_score: float32 [512, 4, 4, 512], P('wind', ('gy', 'gz'), 'gx'), parts along dimension 0
The draws below stay inside these ranges and needn't reach their ends.
There are 2 independent parts, one for each index of `wind`. The reference program is written for one: setup_inputs(seed, part) draws one part's arguments, and reference() takes and returns one part's arrays. A program takes and returns all parts, laid end to end along the dimension named above; an argument that names none is the same for every part. Nothing has to cross between parts.
Inputs may be any that keep to these rules, and one draw needn't show every extreme that they name: `mode_taps`: some mode keeps all 64 taps.
All inputs are finite; a program needn't handle non-finite values.
Results may differ from the reference program's by a relative error of at most 0.005.
Values may be sent and summed in bfloat16 or wider, within the bound.
A program may use at most 64 MiB of HBM per device.

```python
import math
import jax
import jax.numpy as jnp
from jax import lax

TIME = 4096
PAN_DEV = 512
MODES = 256
FIR_TAPS = 257
DYN_TAPS = 64
BLOCKS = 4
GROUPS = 4
PANELS = 8192


def draw_pressure(key, part):
    key_base, key_rows, key_cols = jax.random.split(key, 3)
    half_range = 0.5 * math.log(10.0)
    row_scale = jnp.exp(jax.random.uniform(key_rows, (TIME, 1), jnp.float32, 0.0, half_range))
    col_scale = jnp.exp(jax.random.uniform(key_cols, (1, PANELS), jnp.float32, 0.0, half_range))
    field_values = jax.random.truncated_normal(key_base, -4.0, 4.0, (TIME, PANELS), jnp.float32)
    return (field_values * row_scale * col_scale).astype(jnp.bfloat16)


def draw_mode_taps(key, part):
    key_taps, key_spot = jax.random.split(jax.random.fold_in(key, 7))
    tap_values = jax.random.randint(key_taps, (MODES,), 1, DYN_TAPS + 1, dtype=jnp.int32)
    spot_index = jax.random.randint(key_spot, (), 0, MODES, dtype=jnp.int32)
    return jnp.where(jnp.arange(MODES, dtype=jnp.int32) == spot_index, DYN_TAPS, tap_values).astype(jnp.int32)


def block_scale(rng, extent, cuts, least, largest):
    loudness = 1.0
    for position, shards_of in cuts:
        steps = jax.random.uniform(jax.random.fold_in(jax.random.fold_in(rng, 6), position), (shards_of,), jnp.float32, least / len(cuts), largest / len(cuts))
        loudness = loudness * jnp.repeat(jnp.exp(steps), extent[position] // shards_of).reshape((-1,) + (1,) * (len(extent) - 1 - position))
    return loudness


def bell_draw(stream_key, extent, width, most, cuts=(), held_as=jnp.bfloat16):
    values = width * jax.random.normal(stream_key, extent, jnp.float32)
    if cuts:
        values = values * block_scale(stream_key, extent, cuts, -0.22, 0.18)
    return jnp.clip(values, -most, most).astype(held_as)


def setup_inputs(seed: int = 0, part: int = 0) -> dict:
    keys = jax.random.split(jax.random.key(seed), 6)
    part_splits = jax.random.split(jax.random.fold_in(keys[5], part), 6)
    pressure = draw_pressure(jax.random.fold_in(jax.random.fold_in(keys[5], part), 71), part)
    fir_taps = bell_draw(keys[1], (FIR_TAPS,), FIR_TAPS ** -0.5, 0.375)
    influence = bell_draw(keys[2], (MODES, GROUPS, BLOCKS, PAN_DEV), PANELS ** -0.5, 0.0625, ((1, 4), (2, 4)))
    mode_impulse = bell_draw(keys[3], (MODES, DYN_TAPS), DYN_TAPS ** -0.5, 0.75, (), jnp.float32)
    mode_taps = draw_mode_taps(jax.random.fold_in(keys[5], 71), part)
    return dict(pressure=pressure, fir_taps=fir_taps, influence=influence, mode_impulse=mode_impulse, mode_taps=mode_taps)


def band_matrix(tap_row, row_count):
    tap_count = tap_row.shape[0]
    extended = jnp.concatenate([tap_row[::-1], jnp.zeros((row_count,), tap_row.dtype)])
    tiled_flat = jnp.tile(extended, row_count)[:row_count * (row_count + tap_count - 1)]
    return tiled_flat.reshape(row_count, row_count + tap_count - 1)

def fir_rows(padded_in, tap_row, row_count):
    tap_count = tap_row.shape[0]
    block_rows = min(512, row_count)
    toeplitz = band_matrix(tap_row, block_rows)
    partials = [jnp.dot(toeplitz, padded_in[offset:offset + block_rows + tap_count - 1], preferred_element_type=jnp.float32) for offset in range(0, row_count, block_rows)]
    return jnp.concatenate(partials, axis=0).astype(jnp.bfloat16)

def dynamic_filter(series, impulse, tap_limits):
    impulse_len = impulse.shape[1]
    kept_mask = jnp.arange(impulse_len, dtype=jnp.int32)[None, :] < tap_limits[:, None]
    kernel_taps = jnp.where(kept_mask, impulse, jnp.zeros_like(impulse))[:, ::-1]
    result = lax.conv_general_dilated(series[None], kernel_taps[:, None, :], window_strides=(1,), padding=[(impulse_len - 1, 0)], dimension_numbers=('NCH', 'OIH', 'NCH'), feature_group_count=series.shape[0], precision=lax.Precision.HIGHEST)
    return result[0]

def panel_stats(filtered):
    mean_panel = lax.optimization_barrier(jnp.mean(filtered.astype(jnp.float32), axis=0))
    spread_panel = jnp.sqrt(lax.optimization_barrier(jnp.mean(jnp.square(filtered.astype(jnp.float32) - mean_panel[None, :]), axis=0)) + 1e-06)
    return (mean_panel, spread_panel)

def score_block(responses, filtered, mean_panel, spread_panel):
    sample_count = filtered.shape[0]
    resp_wide = responses.astype(jnp.float32)
    mean_mode = lax.optimization_barrier(jnp.mean(resp_wide, axis=1))
    spread_mode = jnp.sqrt(lax.optimization_barrier(jnp.mean(jnp.square(resp_wide - mean_mode[:, None]), axis=1)) + 1e-06)
    cross = jnp.dot(responses, filtered, preferred_element_type=jnp.float32)
    covariance = cross / sample_count - mean_mode[:, None] * mean_panel[None, :]
    return math.sqrt(sample_count) * covariance / (spread_mode[:, None] * spread_panel[None, :])

def reference(pressure, fir_taps, influence, mode_impulse, mode_taps):
    tap_count = fir_taps.shape[0]
    padded_in = jnp.concatenate([jnp.zeros((tap_count - 1, PANELS), pressure.dtype), pressure], axis=0)
    filtered = fir_rows(padded_in, fir_taps, TIME)
    lines = influence.reshape(MODES, PANELS)
    loads = lax.dot_general(lines, filtered, (((1,), (1,)), ((), ())), preferred_element_type=jnp.float32)
    responses = dynamic_filter(loads, mode_impulse, mode_taps).astype(jnp.bfloat16)
    mean_panel, spread_panel = panel_stats(filtered)
    correlation_score = score_block(responses, filtered, mean_panel, spread_panel).reshape(influence.shape)
    return (responses, correlation_score)
```

```python
import math

import jax
import jax.numpy as jnp
from jax import lax
from jax.sharding import PartitionSpec as P

F32 = jnp.float32
BF16 = jnp.bfloat16


def dot(a, b, contract):
    return lax.dot_general(a, b, (contract, ((), ())), preferred_element_type=F32)


def band_matrix(tap_row, row_count):
    tap_count = tap_row.shape[0]
    extended = jnp.concatenate([tap_row, jnp.zeros((row_count,), tap_row.dtype)])
    flat = jnp.tile(extended, row_count)[: row_count * (row_count + tap_count - 1)]
    return flat.reshape(row_count, row_count + tap_count - 1)


def windows(padded, block, width):
    count = (padded.shape[1] - (width - block)) // block
    return jnp.stack([padded[:, i * block : i * block + width] for i in range(count)], axis=1)


def dynamic_filter(series, impulse, tap_limits):
    impulse_len = impulse.shape[1]
    kept_mask = jnp.arange(impulse_len, dtype=jnp.int32)[None, :] < tap_limits[:, None]
    kernel_taps = jnp.where(kept_mask, impulse, jnp.zeros_like(impulse))[:, ::-1]
    result = lax.conv_general_dilated(
        series[None],
        kernel_taps[:, None, :],
        window_strides=(1,),
        padding=[(impulse_len - 1, 0)],
        dimension_numbers=("NCH", "OIH", "NCH"),
        feature_group_count=series.shape[0],
        precision=lax.Precision.HIGHEST,
    )
    return result[0]


def panel_moments(pressure, halo, band, block):
    rows = pressure.shape[0]
    padded = jnp.concatenate([halo, pressure], axis=0)
    width = band.shape[1]
    parts = [
        dot(band, padded[o : o + width], ((1,), (0,))) for o in range(0, rows, block)
    ]
    filtered = jnp.concatenate(parts, axis=0).astype(BF16)
    wide = filtered.astype(F32)
    mean = jnp.mean(wide, axis=0)
    spread = jnp.sum(jnp.square(wide - mean[None, :]), axis=0)
    return mean, spread


def body(pressure, fir_taps, influence, mode_impulse, mode_taps):
    nx, ng = lax.axis_size("gx"), lax.axis_size(("gy", "gz"))
    rows, panels = pressure.shape
    total = rows * nx
    rim = fir_taps.shape[0] - 1
    modes = influence.shape[0]
    own = modes // (nx * ng)
    own_panels = panels // nx
    block = min(512, rows)

    lines = lax.all_gather(influence.reshape(modes, -1), "gx", axis=1, tiled=True)
    halo = lax.ppermute(pressure[rows - rim :], "gx", [(i, i + 1) for i in range(nx - 1)])

    raw = dot(lines, pressure, ((1,), (1,)))
    raw = lax.psum_scatter(
        raw.reshape(nx, ng * own, rows), ("gy", "gz"), scatter_dimension=1, tiled=True
    )
    raw = lax.all_to_all(raw, "gx", split_axis=0, concat_axis=0, tiled=True)
    raw = raw.transpose(1, 0, 2).reshape(own, total)

    forward = band_matrix(fir_taps, 512)
    backward = band_matrix(fir_taps[::-1], 512)
    width = forward.shape[1]
    padded = jnp.pad(raw, ((0, 0), (rim, 0)))
    high = padded.astype(BF16)
    low = (padded - high.astype(F32)).astype(BF16)
    loads = sum(
        dot(windows(x, 512, width).reshape(-1, width), backward, ((1,), (1,)))
        for x in (high, low)
    ).reshape(own, total)

    first_mode = lax.axis_index(("gx", "gy", "gz")) * own
    own_impulse = lax.dynamic_slice_in_dim(mode_impulse, first_mode, own, 0)
    own_limits = lax.dynamic_slice_in_dim(mode_taps, first_mode, own, 0)
    responses = dynamic_filter(loads, own_impulse, own_limits).astype(BF16)

    resp_wide = responses.astype(F32)
    mean_mode = jnp.mean(resp_wide, axis=1)
    spread_mode = jnp.sqrt(jnp.mean(jnp.square(resp_wide - mean_mode[:, None]), axis=1) + 1e-06)
    ahead = windows(jnp.pad(responses, ((0, 0), (0, rim))), 512, width).reshape(-1, width)
    back = dot(ahead, forward, ((1,), (1,))).reshape(own, total)
    left = total - 1 - jnp.arange(total, dtype=jnp.int32)
    within = jnp.arange(rim + 1, dtype=jnp.int32)[:, None] <= left[None, :]
    reach = jnp.sum(jnp.where(within, fir_taps.astype(F32)[:, None], 0.0), axis=0)
    scale = 1.0 / (math.sqrt(total) * spread_mode)
    back = ((back - mean_mode[:, None] * reach[None, :]) * scale[:, None]).astype(BF16)

    back = back.reshape(own, nx, rows).transpose(1, 0, 2)
    back = lax.all_to_all(back, "gx", split_axis=0, concat_axis=0, tiled=True)
    back = lax.all_gather(back, ("gy", "gz"), axis=1, tiled=True).reshape(modes, rows)

    cross = dot(back, pressure, ((1,), (0,))).astype(BF16)
    cross = lax.all_to_all(
        cross.reshape(modes, nx, own_panels), "gx", split_axis=1, concat_axis=1, tiled=True
    )
    cross = jnp.sum(cross.astype(F32), axis=1)

    mean_part, square_part = panel_moments(
        pressure, halo, band_matrix(fir_taps[::-1], block), block
    )
    moments = jnp.stack([mean_part, square_part]).reshape(2, nx, own_panels)
    moments = lax.all_to_all(moments, "gx", split_axis=1, concat_axis=1, tiled=True)
    mean_panel = jnp.mean(moments[0], axis=0)
    squares = jnp.sum(
        moments[1] + rows * jnp.square(moments[0] - mean_panel[None, :]), axis=0
    )
    spread_panel = jnp.sqrt(squares / total + 1e-06)
    scores = cross / spread_panel[None, :]
    return (responses, scores.reshape(influence.shape))


def solution(mesh):
    return jax.shard_map(
        body,
        mesh=mesh,
        in_specs=(
            P(("wind", "gx"), ("gy", "gz")),
            P(),
            P(None, ("gy", "gz"), "gx", None),
            P(),
            P(),
        ),
        out_specs=(P(("wind", "gx", "gy", "gz"), None), P("wind", ("gy", "gz"), "gx", None)),
        check_vma=False,
    )
```

```python
import functools
import math

import jax
import jax.numpy as jnp
from jax import lax
from jax.experimental import pallas as pl
from jax.experimental.pallas import tpu as pltpu
from jax.sharding import PartitionSpec as P

F32 = jnp.float32
BF16 = jnp.bfloat16


def dot(a, b, contract):
    return lax.dot_general(a, b, (contract, ((), ())), preferred_element_type=F32)


def band_matrix(tap_row, row_count):
    tap_count = tap_row.shape[0]
    extended = jnp.concatenate([tap_row, jnp.zeros((row_count,), tap_row.dtype)])
    flat = jnp.tile(extended, row_count)[: row_count * (row_count + tap_count - 1)]
    return flat.reshape(row_count, row_count + tap_count - 1)


def windows(padded, block, width):
    count = (padded.shape[1] - (width - block)) // block
    return jnp.stack([padded[:, i * block : i * block + width] for i in range(count)], axis=1)


def dynamic_filter(series, impulse, tap_limits):
    impulse_len = impulse.shape[1]
    kept_mask = jnp.arange(impulse_len, dtype=jnp.int32)[None, :] < tap_limits[:, None]
    kernel_taps = jnp.where(kept_mask, impulse, jnp.zeros_like(impulse))[:, ::-1]
    result = lax.conv_general_dilated(
        series[None],
        kernel_taps[:, None, :],
        window_strides=(1,),
        padding=[(impulse_len - 1, 0)],
        dimension_numbers=("NCH", "OIH", "NCH"),
        feature_group_count=series.shape[0],
        precision=lax.Precision.HIGHEST,
    )
    return result[0]


def panel_moments(pressure, halo, band, block):
    rows = pressure.shape[0]
    padded = jnp.concatenate([halo, pressure], axis=0)
    width = band.shape[1]
    parts = [
        dot(band, padded[o : o + width], ((1,), (0,))) for o in range(0, rows, block)
    ]
    filtered = jnp.concatenate(parts, axis=0).astype(BF16)
    wide = filtered.astype(F32)
    mean = jnp.mean(wide, axis=0)
    spread = jnp.sum(jnp.square(wide - mean[None, :]), axis=0)
    return mean, spread


def plain_body(pressure, fir_taps, influence, mode_impulse, mode_taps):
    nx, ng = lax.axis_size("gx"), lax.axis_size(("gy", "gz"))
    rows, panels = pressure.shape
    total = rows * nx
    rim = fir_taps.shape[0] - 1
    modes = influence.shape[0]
    own = modes // (nx * ng)
    own_panels = panels // nx
    block = min(512, rows)

    lines = lax.all_gather(influence.reshape(modes, -1), "gx", axis=1, tiled=True)
    halo = lax.ppermute(pressure[rows - rim :], "gx", [(i, i + 1) for i in range(nx - 1)])

    raw = dot(lines, pressure, ((1,), (1,)))
    raw = lax.psum_scatter(
        raw.reshape(nx, ng * own, rows), ("gy", "gz"), scatter_dimension=1, tiled=True
    )
    raw = lax.all_to_all(raw, "gx", split_axis=0, concat_axis=0, tiled=True)
    raw = raw.transpose(1, 0, 2).reshape(own, total)

    forward = band_matrix(fir_taps, 512)
    backward = band_matrix(fir_taps[::-1], 512)
    width = forward.shape[1]
    padded = jnp.pad(raw, ((0, 0), (rim, 0)))
    high = padded.astype(BF16)
    low = (padded - high.astype(F32)).astype(BF16)
    loads = sum(
        dot(windows(x, 512, width).reshape(-1, width), backward, ((1,), (1,)))
        for x in (high, low)
    ).reshape(own, total)

    first_mode = lax.axis_index(("gx", "gy", "gz")) * own
    own_impulse = lax.dynamic_slice_in_dim(mode_impulse, first_mode, own, 0)
    own_limits = lax.dynamic_slice_in_dim(mode_taps, first_mode, own, 0)
    responses = dynamic_filter(loads, own_impulse, own_limits).astype(BF16)

    resp_wide = responses.astype(F32)
    mean_mode = jnp.mean(resp_wide, axis=1)
    spread_mode = jnp.sqrt(jnp.mean(jnp.square(resp_wide - mean_mode[:, None]), axis=1) + 1e-06)
    ahead = windows(jnp.pad(responses, ((0, 0), (0, rim))), 512, width).reshape(-1, width)
    back = dot(ahead, forward, ((1,), (1,))).reshape(own, total)
    left = total - 1 - jnp.arange(total, dtype=jnp.int32)
    within = jnp.arange(rim + 1, dtype=jnp.int32)[:, None] <= left[None, :]
    reach = jnp.sum(jnp.where(within, fir_taps.astype(F32)[:, None], 0.0), axis=0)
    scale = 1.0 / (math.sqrt(total) * spread_mode)
    back = ((back - mean_mode[:, None] * reach[None, :]) * scale[:, None]).astype(BF16)

    back = back.reshape(own, nx, rows).transpose(1, 0, 2)
    back = lax.all_to_all(back, "gx", split_axis=0, concat_axis=0, tiled=True)
    back = lax.all_gather(back, ("gy", "gz"), axis=1, tiled=True).reshape(modes, rows)

    cross = dot(back, pressure, ((1,), (0,))).astype(BF16)
    cross = lax.all_to_all(
        cross.reshape(modes, nx, own_panels), "gx", split_axis=1, concat_axis=1, tiled=True
    )
    cross = jnp.sum(cross.astype(F32), axis=1)

    mean_part, square_part = panel_moments(
        pressure, halo, band_matrix(fir_taps[::-1], block), block
    )
    moments = jnp.stack([mean_part, square_part]).reshape(2, nx, own_panels)
    moments = lax.all_to_all(moments, "gx", split_axis=1, concat_axis=1, tiled=True)
    mean_panel = jnp.mean(moments[0], axis=0)
    squares = jnp.sum(
        moments[1] + rows * jnp.square(moments[0] - mean_panel[None, :]), axis=0
    )
    spread_panel = jnp.sqrt(squares / total + 1e-06)
    scores = cross / spread_panel[None, :]
    return (responses, scores.reshape(influence.shape))


SPAN = 512
LEAD = 128
COLS = 256


def tower_kernel(
    nx, own, dyn, infl, press, taps, gains, resp, score,
    lines, raw, from_core, core_sum, from_pair, pair_sum, slots, series, loads, wide_gain,
    modal, band_back, band_fwd, halo, filt, turned, back, part, arrived, moments, moved,
    send, recv,
):
    rows, panels = press.shape
    modes, own_panels = infl.shape
    total = rows * nx
    rim = halo.shape[0]
    spans = total // SPAN
    gx, gy, gz = lax.axis_index("gx"), lax.axis_index("gy"), lax.axis_index("gz")
    mesh_id = pl.DeviceIdType.MESH

    def remote(src, dst, sem, device):
        return pltpu.make_async_remote_copy(
            src_ref=src, dst_ref=dst, send_sem=send.at[sem], recv_sem=recv.at[sem],
            device_id=device, device_id_type=mesh_id,
        )

    def ahead(d):
        return lax.rem(gx + d, nx)

    def behind(d):
        return lax.rem(gx + nx - d, nx)

    def columns(index, size):
        return pl.ds(pl.multiple_of(index * size, size), size)

    hops = range(1, nx)
    first = {name: i * nx for i, name in enumerate(("lines", "raw", "back", "cross", "moments"))}
    extra = 5 * nx

    barrier = pltpu.get_barrier_semaphore()
    peers = [{"gx": ahead(d)} for d in hops] + [{"gy": 1 - gy}, {"gz": 1 - gz}]
    for peer in peers:
        pl.semaphore_signal(barrier, inc=1, device_id=peer, device_id_type=mesh_id)
    pl.semaphore_wait(barrier, len(peers))

    line_copies = [
        remote(infl, lines.at[d], first["lines"] + d, {"gx": ahead(d)}) for d in hops
    ]
    for copy in line_copies:
        copy.start()
    halo_copy = remote(press.at[pl.ds(rows - rim, rim)], halo, extra, {"gx": ahead(1)})

    width = band_back.shape[1]
    for c in range(SPAN // LEAD):
        for k, band in ((0, band_fwd), (1, band_back)):
            line = jnp.broadcast_to(taps[pl.ds(k, 1), :], (LEAD, width))
            band[pl.ds(c * LEAD, LEAD), :] = pltpu.roll(
                line, c * LEAD, 1, stride=1, stride_axis=0
            ).astype(BF16)
    for k in range(dyn):
        wide_gain[k] = jnp.broadcast_to(gains[:, k : k + 1], (own, LEAD))
    series[:, pl.ds(0, rim)] = jnp.zeros((own, rim), F32)
    loads[:, pl.ds(0, LEAD)] = jnp.zeros((own, LEAD), F32)
    modal[:, pl.ds(total, rim)] = jnp.zeros((own, rim), BF16)
    moments[...] = jnp.zeros(moments.shape, F32)

    @pl.when(gx == 0)
    def _():
        halo[...] = jnp.zeros(halo.shape, BF16)

    def add_lines(block, held, fresh):
        def step(i, _):
            at = columns(i, COLS)
            piece = press[at, columns(block, own_panels)]
            term = dot(held[...], piece, ((1,), (1,))).reshape(nx, 2, 2, own, COLS)
            if fresh:
                raw[:, :, :, :, at] = term
            else:
                raw[:, :, :, :, at] += term
            return 0

        lax.fori_loop(0, rows // COLS, step, 0)

    add_lines(gx, infl, True)

    def filter_later(i, _):
        at = columns(i, COLS)
        for o in range(SPAN, rows, SPAN):
            piece = press[pl.ds(o - rim, SPAN + rim), at]
            filt[pl.ds(o, SPAN), at] = dot(band_back[...], piece, ((1,), (0,))).astype(BF16)
        return 0

    lax.fori_loop(0, panels // COLS, filter_later, 0)

    for d, copy in zip(hops, line_copies):
        copy.wait_recv()
        add_lines(behind(d), lines.at[d], False)

    core_copy = remote(raw.at[:, :, 1 - gz], from_core, extra + 1, {"gz": 1 - gz})
    core_copy.start()
    core_copy.wait_recv()
    core_sum[...] = raw[:, :, gz] + from_core[...]
    pair_copy = remote(core_sum.at[:, 1 - gy], from_pair, extra + 2, {"gy": 1 - gy})
    pair_copy.start()
    pair_copy.wait_recv()
    pair_sum[...] = core_sum[:, gy] + from_pair[...]
    raw_copies = [
        remote(pair_sum.at[ahead(d)], slots.at[d], first["raw"] + d, {"gx": ahead(d)})
        for d in hops
    ]
    for copy in raw_copies:
        copy.start()

    @pl.when(gx < nx - 1)
    def _():
        halo_copy.start()

    def place(block):
        return pl.ds(pl.multiple_of(block * rows + rim, LEAD), rows)

    series[:, place(gx)] = pair_sum[gx]
    for d, copy in zip(hops, raw_copies):
        copy.wait_recv()
        series[:, place(behind(d))] = slots[d]

    high, low = [], []
    for i in range(spans):
        piece = series[:, pl.ds(i * SPAN, SPAN + rim)]
        top = piece.astype(BF16)
        high.append(top)
        low.append((piece - top.astype(F32)).astype(BF16))
    both = dot(jnp.concatenate(high + low, axis=0), band_back[...], ((1,), (1,)))
    for i in range(spans):
        loads[:, pl.ds(LEAD + i * SPAN, SPAN)] = (
            both[i * own : (i + 1) * own] + both[(spans + i) * own : (spans + i + 1) * own]
        )

    def respond(i, _):
        piece = loads[:, pl.ds(pl.multiple_of(i * SPAN, SPAN), SPAN + LEAD)]
        result = jnp.zeros((own, SPAN), F32)
        for k in range(dyn):
            gain = jnp.concatenate([wide_gain[k]] * (SPAN // LEAD), axis=1)
            moved_by = piece if k == 0 else pltpu.roll(piece, k, 1)
            result = result + gain * moved_by[:, LEAD:]
        modal[:, columns(i, SPAN)] = result.astype(BF16)
        return 0

    lax.fori_loop(0, spans, respond, 0)

    settled = modal[:, pl.ds(0, total)]
    resp[...] = settled
    wide = settled.astype(F32)
    mean_mode = jnp.mean(wide, axis=1, keepdims=True)
    off = wide - mean_mode
    spread_mode = jnp.sqrt(jnp.mean(off * off, axis=1, keepdims=True) + 1e-06)
    scale = 1.0 / (math.sqrt(total) * spread_mode)

    later = [modal[:, pl.ds(i * SPAN, SPAN + rim)] for i in range(spans)]
    lane = lax.broadcasted_iota(jnp.int32, (own, width), 1)
    full = jnp.ones((own, width), F32).astype(BF16)
    cut = jnp.where(lane < SPAN, 1.0, 0.0).astype(BF16)
    turned_wide = dot(jnp.concatenate(later + [full, cut], axis=0), band_fwd[...], ((1,), (1,)))
    reach = [turned_wide[(spans + j) * own : (spans + j + 1) * own] for j in range(2)]
    for i in range(spans):
        value = turned_wide[i * own : (i + 1) * own] - mean_mode * reach[int(i == spans - 1)]
        block, offset = divmod(i * SPAN, rows)
        turned[block, :, pl.ds(offset, SPAN)] = (value * scale).astype(BF16)

    back_copies = [
        remote(turned.at[ahead(d)], back.at[gx, gy, gz], first["back"] + d, {"gx": ahead(d)})
        for d in hops
    ]
    for copy in back_copies:
        copy.start()
    back[gx, gy, gz] = turned[gx]

    @pl.when(gx > 0)
    def _():
        halo_copy.wait_recv()

    def filter_first(i, _):
        at = columns(i, COLS)
        value = dot(band_back[:, pl.ds(0, rim)], halo[:, at], ((1,), (0,)))
        value += dot(band_back[:, pl.ds(rim, SPAN)], press[pl.ds(0, SPAN), at], ((1,), (0,)))
        filt[pl.ds(0, SPAN), at] = value.astype(BF16)
        return 0

    def measure(block, slot):
        for j in range(own_panels // COLS):
            at = pl.ds(pl.multiple_of(block * own_panels + j * COLS, COLS), COLS)
            values = filt[:, at].astype(F32)
            mean = jnp.mean(values, axis=0, keepdims=True)
            gap = values - mean
            moments[slot, pl.ds(0, 1), pl.ds(j * COLS, COLS)] = mean
            moments[slot, pl.ds(1, 1), pl.ds(j * COLS, COLS)] = jnp.sum(
                gap * gap, axis=0, keepdims=True
            )

    lax.fori_loop(0, panels // COLS, filter_first, 0)
    moment_copies = []
    for d in range(nx):
        measure(ahead(d), d)
        if d:
            copy = remote(moments.at[d], moved.at[d], first["moments"] + d, {"gx": ahead(d)})
            copy.start()
            moment_copies.append(copy)

    for copy in back_copies:
        copy.wait_recv()
    mine = back.at[:, gy, gz]
    back_pair = remote(mine, mine, extra + 3, {"gy": 1 - gy})
    back_core = remote(mine, mine, extra + 4, {"gz": 1 - gz})
    back_pair.start()
    back_core.start()
    back_pair.wait_recv()
    other = back.at[:, 1 - gy, gz]
    back_forward = remote(other, other, extra + 5, {"gz": 1 - gz})
    back_forward.start()
    back_core.wait_recv()
    back_forward.wait_recv()

    def cross_block(block, j):
        at = pl.ds(pl.multiple_of(block * own_panels + j * COLS, COLS), COLS)
        return dot(back[...].reshape(modes, rows), press[:, at], ((1,), (0,)))

    cross_copies = []
    for d in hops:
        for j in range(own_panels // COLS):
            part[d, :, pl.ds(j * COLS, COLS)] = cross_block(ahead(d), j).astype(BF16)
        copy = remote(part.at[d], arrived.at[d], first["cross"] + d, {"gx": ahead(d)})
        copy.start()
        cross_copies.append(copy)
    for j in range(own_panels // COLS):
        score[:, pl.ds(j * COLS, COLS)] = cross_block(gx, j)

    for copy in moment_copies:
        copy.wait_recv()
    means = [moments[0, pl.ds(0, 1), :]] + [moved[d, pl.ds(0, 1), :] for d in hops]
    squares = [moments[0, pl.ds(1, 1), :]] + [moved[d, pl.ds(1, 1), :] for d in hops]
    mean_panel = sum(means) / nx
    spread = sum(squares) + rows * sum(jnp.square(m - mean_panel) for m in means)
    factor = 1.0 / jnp.sqrt(spread / total + 1e-06)
    for copy in cross_copies:
        copy.wait_recv()
    value = score[...]
    for d in hops:
        value = value + arrived[d].astype(F32)
    score[...] = value * factor

    for copy in line_copies + raw_copies + back_copies + moment_copies + cross_copies:
        copy.wait_send()
    for copy in (core_copy, pair_copy, back_pair, back_core, back_forward):
        copy.wait_send()

    @pl.when(gx < nx - 1)
    def _():
        halo_copy.wait_send()


def body(pressure, fir_taps, influence, mode_impulse, mode_taps):
    nx, ny, nz = (lax.axis_size(name) for name in ("gx", "gy", "gz"))
    rows, panels = pressure.shape
    total = rows * nx
    rim = fir_taps.shape[0] - 1
    modes = influence.shape[0]
    own = modes // (nx * ny * nz)
    own_panels = panels // nx
    dyn = mode_impulse.shape[1]
    fits = own % 16 == 0 and ny == nz == 2 and rows % SPAN == 0 and own_panels % COLS == 0
    if not fits or rim % LEAD or dyn > LEAD:
        return plain_body(pressure, fir_taps, influence, mode_impulse, mode_taps)

    first_mode = lax.axis_index(("gx", "gy", "gz")) * own
    own_impulse = lax.dynamic_slice_in_dim(mode_impulse, first_mode, own, 0)
    own_limits = lax.dynamic_slice_in_dim(mode_taps, first_mode, own, 0)
    kept = jnp.arange(dyn, dtype=jnp.int32)[None, :] < own_limits[:, None]
    gains = jnp.where(kept, own_impulse, 0.0)
    width = SPAN + rim
    tap_rows = jnp.stack([fir_taps, fir_taps[::-1]]).astype(F32)
    tap_rows = jnp.pad(tap_rows, ((0, 0), (0, width - rim - 1)))

    vmem = pl.BlockSpec(memory_space=pltpu.VMEM)
    responses, scores = pl.pallas_call(
        functools.partial(tower_kernel, nx, own, dyn),
        out_shape=(
            jax.ShapeDtypeStruct((own, total), BF16),
            jax.ShapeDtypeStruct((modes, own_panels), F32),
        ),
        in_specs=[vmem] * 4,
        out_specs=(vmem, vmem),
        scratch_shapes=[
            pltpu.VMEM((nx, modes, own_panels), BF16),
            pltpu.VMEM((nx, 2, 2, own, rows), F32),
            pltpu.VMEM((nx, 2, own, rows), F32),
            pltpu.VMEM((nx, 2, own, rows), F32),
            pltpu.VMEM((nx, own, rows), F32),
            pltpu.VMEM((nx, own, rows), F32),
            pltpu.VMEM((nx, own, rows), F32),
            pltpu.VMEM((own, rim + total), F32),
            pltpu.VMEM((own, LEAD + total), F32),
            pltpu.VMEM((dyn, own, LEAD), F32),
            pltpu.VMEM((own, total + rim), BF16),
            pltpu.VMEM((SPAN, width), BF16),
            pltpu.VMEM((SPAN, width), BF16),
            pltpu.VMEM((rim, panels), BF16),
            pltpu.VMEM((rows, panels), BF16),
            pltpu.VMEM((nx, own, rows), BF16),
            pltpu.VMEM((nx, 2, 2, own, rows), BF16),
            pltpu.VMEM((nx, modes, own_panels), BF16),
            pltpu.VMEM((nx, modes, own_panels), BF16),
            pltpu.VMEM((nx, 8, own_panels), F32),
            pltpu.VMEM((nx, 8, own_panels), F32),
            pltpu.SemaphoreType.DMA((5 * nx + 6,)),
            pltpu.SemaphoreType.DMA((5 * nx + 6,)),
        ],
        compiler_params=pltpu.CompilerParams(
            collective_id=0, has_side_effects=True, vmem_limit_bytes=48 * 1024 * 1024
        ),
    )(influence.reshape(modes, own_panels), pressure, tap_rows, gains)
    return responses, scores.reshape(influence.shape)


def solution(mesh):
    return jax.shard_map(
        body,
        mesh=mesh,
        in_specs=(
            P(("wind", "gx"), ("gy", "gz")),
            P(),
            P(None, ("gy", "gz"), "gx", None),
            P(),
            P(),
        ),
        out_specs=(P(("wind", "gx", "gy", "gz"), None), P("wind", ("gy", "gz"), "gx", None)),
        check_vma=False,
    )
```

```python
import functools
import math

import jax
import jax.numpy as jnp
from jax import lax
from jax.experimental import pallas as pl
from jax.experimental.pallas import tpu as pltpu
from jax.sharding import PartitionSpec as P

F32 = jnp.float32
BF16 = jnp.bfloat16


def dot(a, b, contract):
    return lax.dot_general(a, b, (contract, ((), ())), preferred_element_type=F32)


def band_matrix(tap_row, row_count):
    tap_count = tap_row.shape[0]
    extended = jnp.concatenate([tap_row, jnp.zeros((row_count,), tap_row.dtype)])
    flat = jnp.tile(extended, row_count)[: row_count * (row_count + tap_count - 1)]
    return flat.reshape(row_count, row_count + tap_count - 1)


def windows(padded, block, width):
    count = (padded.shape[1] - (width - block)) // block
    return jnp.stack([padded[:, i * block : i * block + width] for i in range(count)], axis=1)


def dynamic_filter(series, impulse, tap_limits):
    impulse_len = impulse.shape[1]
    kept_mask = jnp.arange(impulse_len, dtype=jnp.int32)[None, :] < tap_limits[:, None]
    kernel_taps = jnp.where(kept_mask, impulse, jnp.zeros_like(impulse))[:, ::-1]
    result = lax.conv_general_dilated(
        series[None],
        kernel_taps[:, None, :],
        window_strides=(1,),
        padding=[(impulse_len - 1, 0)],
        dimension_numbers=("NCH", "OIH", "NCH"),
        feature_group_count=series.shape[0],
        precision=lax.Precision.HIGHEST,
    )
    return result[0]


def panel_moments(pressure, halo, band, block):
    rows = pressure.shape[0]
    padded = jnp.concatenate([halo, pressure], axis=0)
    width = band.shape[1]
    parts = [
        dot(band, padded[o : o + width], ((1,), (0,))) for o in range(0, rows, block)
    ]
    filtered = jnp.concatenate(parts, axis=0).astype(BF16)
    wide = filtered.astype(F32)
    mean = jnp.mean(wide, axis=0)
    spread = jnp.sum(jnp.square(wide - mean[None, :]), axis=0)
    return mean, spread


def plain_body(pressure, fir_taps, influence, mode_impulse, mode_taps):
    nx, ng = lax.axis_size("gx"), lax.axis_size(("gy", "gz"))
    rows, panels = pressure.shape
    total = rows * nx
    rim = fir_taps.shape[0] - 1
    modes = influence.shape[0]
    own = modes // (nx * ng)
    own_panels = panels // nx
    block = min(512, rows)

    lines = lax.all_gather(influence.reshape(modes, -1), "gx", axis=1, tiled=True)
    halo = lax.ppermute(pressure[rows - rim :], "gx", [(i, i + 1) for i in range(nx - 1)])

    raw = dot(lines, pressure, ((1,), (1,)))
    raw = lax.psum_scatter(
        raw.reshape(nx, ng * own, rows), ("gy", "gz"), scatter_dimension=1, tiled=True
    )
    raw = lax.all_to_all(raw, "gx", split_axis=0, concat_axis=0, tiled=True)
    raw = raw.transpose(1, 0, 2).reshape(own, total)

    forward = band_matrix(fir_taps, 512)
    backward = band_matrix(fir_taps[::-1], 512)
    width = forward.shape[1]
    padded = jnp.pad(raw, ((0, 0), (rim, 0)))
    high = padded.astype(BF16)
    low = (padded - high.astype(F32)).astype(BF16)
    loads = sum(
        dot(windows(x, 512, width).reshape(-1, width), backward, ((1,), (1,)))
        for x in (high, low)
    ).reshape(own, total)

    first_mode = lax.axis_index(("gx", "gy", "gz")) * own
    own_impulse = lax.dynamic_slice_in_dim(mode_impulse, first_mode, own, 0)
    own_limits = lax.dynamic_slice_in_dim(mode_taps, first_mode, own, 0)
    responses = dynamic_filter(loads, own_impulse, own_limits).astype(BF16)

    resp_wide = responses.astype(F32)
    mean_mode = jnp.mean(resp_wide, axis=1)
    spread_mode = jnp.sqrt(jnp.mean(jnp.square(resp_wide - mean_mode[:, None]), axis=1) + 1e-06)
    ahead = windows(jnp.pad(responses, ((0, 0), (0, rim))), 512, width).reshape(-1, width)
    back = dot(ahead, forward, ((1,), (1,))).reshape(own, total)
    left = total - 1 - jnp.arange(total, dtype=jnp.int32)
    within = jnp.arange(rim + 1, dtype=jnp.int32)[:, None] <= left[None, :]
    reach = jnp.sum(jnp.where(within, fir_taps.astype(F32)[:, None], 0.0), axis=0)
    scale = 1.0 / (math.sqrt(total) * spread_mode)
    back = ((back - mean_mode[:, None] * reach[None, :]) * scale[:, None]).astype(BF16)

    back = back.reshape(own, nx, rows).transpose(1, 0, 2)
    back = lax.all_to_all(back, "gx", split_axis=0, concat_axis=0, tiled=True)
    back = lax.all_gather(back, ("gy", "gz"), axis=1, tiled=True).reshape(modes, rows)

    cross = dot(back, pressure, ((1,), (0,))).astype(BF16)
    cross = lax.all_to_all(
        cross.reshape(modes, nx, own_panels), "gx", split_axis=1, concat_axis=1, tiled=True
    )
    cross = jnp.sum(cross.astype(F32), axis=1)

    mean_part, square_part = panel_moments(
        pressure, halo, band_matrix(fir_taps[::-1], block), block
    )
    moments = jnp.stack([mean_part, square_part]).reshape(2, nx, own_panels)
    moments = lax.all_to_all(moments, "gx", split_axis=1, concat_axis=1, tiled=True)
    mean_panel = jnp.mean(moments[0], axis=0)
    squares = jnp.sum(
        moments[1] + rows * jnp.square(moments[0] - mean_panel[None, :]), axis=0
    )
    spread_panel = jnp.sqrt(squares / total + 1e-06)
    scores = cross / spread_panel[None, :]
    return (responses, scores.reshape(influence.shape))


SPAN = 512
LEAD = 128
COLS = 256


def tower_kernel(
    nx, own, dyn, infl, outside, taps, gains, resp, score, press, fetched,
    lines, raw, from_core, core_sum, from_pair, pair_sum, slots, series, loads, wide_gain,
    modal, band_back, band_fwd, halo, filt, turned, back, part, arrived, moments, moved,
    send, recv,
):
    rows, panels = press.shape
    modes, own_panels = infl.shape
    total = rows * nx
    rim = halo.shape[0]
    spans = total // SPAN
    wind = lax.axis_index("wind")
    gx, gy, gz = lax.axis_index("gx"), lax.axis_index("gy"), lax.axis_index("gz")
    mesh_id = pl.DeviceIdType.MESH

    def remote(src, dst, sem, device):
        return pltpu.make_async_remote_copy(
            src_ref=src, dst_ref=dst, send_sem=send.at[sem], recv_sem=recv.at[sem],
            device_id=device, device_id_type=mesh_id,
        )

    def ahead(d):
        return lax.rem(gx + d, nx)

    def behind(d):
        return lax.rem(gx + nx - d, nx)

    def columns(index, size):
        return pl.ds(pl.multiple_of(index * size, size), size)

    hops = range(1, nx)
    first = {name: i * nx for i, name in enumerate(("lines", "raw", "back", "cross", "moments", "twin"))}
    extra = 6 * nx

    fetch = pltpu.make_async_copy(outside, press, fetched)
    fetch.start()
    barrier = pltpu.get_barrier_semaphore()
    peers = [{"gx": ahead(d)} for d in hops] + [{"gy": 1 - gy}, {"gz": 1 - gz}, {"wind": 1 - wind}]
    for peer in peers:
        pl.semaphore_signal(barrier, inc=1, device_id=peer, device_id_type=mesh_id)
    pl.semaphore_wait(barrier, len(peers))

    share = columns(wind, modes // 2)
    line_copies = [
        remote(infl.at[share], lines.at[d, share], first["lines"] + d, {"gx": ahead(d)})
        for d in hops
    ]
    twin_copies = [
        remote(lines.at[d, share], lines.at[d, share], first["twin"] + d, {"wind": 1 - wind})
        for d in hops
    ]
    for copy in line_copies:
        copy.start()
    halo_copy = remote(press.at[pl.ds(rows - rim, rim)], halo, extra, {"gx": ahead(1)})

    width = band_back.shape[1]
    reach_to = rim + LEAD
    cross_sum = lax.broadcasted_iota(jnp.int32, (reach_to, reach_to), 0)
    cross_sum += lax.broadcasted_iota(jnp.int32, (reach_to, reach_to), 1)
    flip = jnp.where(cross_sum == rim, 1.0, 0.0).astype(BF16)
    reverse = dot(taps[:, pl.ds(0, reach_to)], flip, ((1,), (0,)))[0:1]
    reverse = jnp.concatenate([reverse, jnp.zeros((1, width - reach_to), F32)], axis=1)
    tap_line = taps[...].astype(F32)[0:1]
    for c in range(SPAN // LEAD):
        for tap_row, band in ((tap_line, band_fwd), (reverse, band_back)):
            line = jnp.broadcast_to(tap_row, (LEAD, width))
            band[pl.ds(c * LEAD, LEAD), :] = pltpu.roll(
                line, c * LEAD, 1, stride=1, stride_axis=0
            ).astype(BF16)
    for k in range(dyn):
        wide_gain[k] = jnp.broadcast_to(gains[:, k : k + 1], (own, LEAD))
    series[:, pl.ds(0, rim)] = jnp.zeros((own, rim), F32)
    loads[:, pl.ds(0, LEAD)] = jnp.zeros((own, LEAD), F32)
    modal[:, pl.ds(total, rim)] = jnp.zeros((own, rim), BF16)
    moments[...] = jnp.zeros(moments.shape, F32)

    @pl.when(gx == 0)
    def _():
        halo[...] = jnp.zeros(halo.shape, BF16)

    def add_lines(block, held, fresh):
        def step(i, _):
            at = columns(i, COLS)
            piece = press[at, columns(block, own_panels)]
            term = dot(held[...], piece, ((1,), (1,))).reshape(nx, 2, 2, own, COLS)
            if fresh:
                raw[:, :, :, :, at] = term
            else:
                raw[:, :, :, :, at] += term
            return 0

        lax.fori_loop(0, rows // COLS, step, 0)

    fetch.wait()
    add_lines(gx, infl, True)

    def filter_later(i, _):
        at = columns(i, COLS)
        for o in range(SPAN, rows, SPAN):
            piece = press[pl.ds(o - rim, SPAN + rim), at]
            filt[pl.ds(o, SPAN), at] = dot(band_back[...], piece, ((1,), (0,))).astype(BF16)
        return 0

    lax.fori_loop(0, panels // COLS, filter_later, 0)

    order = sorted(hops, key=lambda d: min(d, nx - d))
    for d in order:
        line_copies[d - 1].wait_recv()
        twin_copies[d - 1].start()
    for d in order:
        twin_copies[d - 1].wait_recv()
        add_lines(behind(d), lines.at[d], False)

    @pl.when(gx < nx - 1)
    def _():
        halo_copy.start()

    core_copy = remote(raw.at[:, :, 1 - gz], from_core, extra + 1, {"gz": 1 - gz})
    core_copy.start()
    core_copy.wait_recv()
    core_sum[...] = raw[:, :, gz] + from_core[...]
    pair_copy = remote(core_sum.at[:, 1 - gy], from_pair, extra + 2, {"gy": 1 - gy})
    pair_copy.start()
    pair_copy.wait_recv()
    pair_sum[...] = core_sum[:, gy] + from_pair[...]
    raw_copies = [
        remote(pair_sum.at[ahead(d)], slots.at[d], first["raw"] + d, {"gx": ahead(d)})
        for d in hops
    ]
    for copy in raw_copies:
        copy.start()

    def place(block):
        return pl.ds(pl.multiple_of(block * rows + rim, LEAD), rows)

    series[:, place(gx)] = pair_sum[gx]
    for d, copy in zip(hops, raw_copies):
        copy.wait_recv()
        series[:, place(behind(d))] = slots[d]

    high, low = [], []
    for i in range(spans):
        piece = series[:, pl.ds(i * SPAN, SPAN + rim)]
        top = piece.astype(BF16)
        high.append(top)
        low.append((piece - top.astype(F32)).astype(BF16))
    both = dot(jnp.concatenate(high + low, axis=0), band_back[...], ((1,), (1,)))
    for i in range(spans):
        loads[:, pl.ds(LEAD + i * SPAN, SPAN)] = (
            both[i * own : (i + 1) * own] + both[(spans + i) * own : (spans + i + 1) * own]
        )

    def respond(i, _):
        piece = loads[:, pl.ds(pl.multiple_of(i * SPAN, SPAN), SPAN + LEAD)]
        result = jnp.zeros((own, SPAN), F32)
        for k in range(dyn):
            gain = jnp.concatenate([wide_gain[k]] * (SPAN // LEAD), axis=1)
            moved_by = piece if k == 0 else pltpu.roll(piece, k, 1)
            result = result + gain * moved_by[:, LEAD:]
        modal[:, columns(i, SPAN)] = result.astype(BF16)
        return 0

    lax.fori_loop(0, spans, respond, 0)

    settled = modal[:, pl.ds(0, total)]
    resp[...] = settled
    wide = settled.astype(F32)
    mean_mode = jnp.mean(wide, axis=1, keepdims=True)
    off = wide - mean_mode
    spread_mode = jnp.sqrt(jnp.mean(off * off, axis=1, keepdims=True) + 1e-06)
    scale = 1.0 / (math.sqrt(total) * spread_mode)

    later = [modal[:, pl.ds(i * SPAN, SPAN + rim)] for i in range(spans)]
    lane = lax.broadcasted_iota(jnp.int32, (own, width), 1)
    full = jnp.ones((own, width), F32).astype(BF16)
    cut = jnp.where(lane < SPAN, 1.0, 0.0).astype(BF16)
    turned_wide = dot(jnp.concatenate(later + [full, cut], axis=0), band_fwd[...], ((1,), (1,)))
    reach = [turned_wide[(spans + j) * own : (spans + j + 1) * own] for j in range(2)]
    for i in range(spans):
        value = turned_wide[i * own : (i + 1) * own] - mean_mode * reach[int(i == spans - 1)]
        block, offset = divmod(i * SPAN, rows)
        turned[block, :, pl.ds(offset, SPAN)] = (value * scale).astype(BF16)

    back_copies = [
        remote(turned.at[ahead(d)], back.at[gx, gy, gz], first["back"] + d, {"gx": ahead(d)})
        for d in hops
    ]
    for copy in back_copies:
        copy.start()
    back[gx, gy, gz] = turned[gx]

    for copy in back_copies:
        copy.wait_recv()
    mine = back.at[:, gy, gz]
    back_pair = remote(mine, mine, extra + 3, {"gy": 1 - gy})
    back_core = remote(mine, mine, extra + 4, {"gz": 1 - gz})
    back_pair.start()
    back_core.start()
    back_pair.wait_recv()
    other = back.at[:, 1 - gy, gz]
    back_forward = remote(other, other, extra + 5, {"gz": 1 - gz})
    back_forward.start()
    back_core.wait_recv()
    back_forward.wait_recv()

    def cross_block(block, j):
        at = pl.ds(pl.multiple_of(block * own_panels + j * COLS, COLS), COLS)
        return dot(back[...].reshape(modes, rows), press[:, at], ((1,), (0,)))

    cross_copies = []
    for d in hops:
        for j in range(own_panels // COLS):
            part[d, :, pl.ds(j * COLS, COLS)] = cross_block(ahead(d), j).astype(BF16)
        copy = remote(part.at[d], arrived.at[d], first["cross"] + d, {"gx": ahead(d)})
        copy.start()
        cross_copies.append(copy)
    for j in range(own_panels // COLS):
        score[:, pl.ds(j * COLS, COLS)] = cross_block(gx, j)

    @pl.when(gx > 0)
    def _():
        halo_copy.wait_recv()

    def filter_first(i, _):
        at = columns(i, COLS)
        value = dot(band_back[:, pl.ds(0, rim)], halo[:, at], ((1,), (0,)))
        value += dot(band_back[:, pl.ds(rim, SPAN)], press[pl.ds(0, SPAN), at], ((1,), (0,)))
        filt[pl.ds(0, SPAN), at] = value.astype(BF16)
        return 0

    def measure(block, slot):
        for j in range(own_panels // COLS):
            at = pl.ds(pl.multiple_of(block * own_panels + j * COLS, COLS), COLS)
            values = filt[:, at].astype(F32)
            mean = jnp.mean(values, axis=0, keepdims=True)
            gap = values - mean
            moments[slot, pl.ds(0, 1), pl.ds(j * COLS, COLS)] = mean
            moments[slot, pl.ds(1, 1), pl.ds(j * COLS, COLS)] = jnp.sum(
                gap * gap, axis=0, keepdims=True
            )

    lax.fori_loop(0, panels // COLS, filter_first, 0)
    moment_copies = []
    for d in range(nx):
        measure(ahead(d), d)
        if d:
            copy = remote(moments.at[d], moved.at[d], first["moments"] + d, {"gx": ahead(d)})
            copy.start()
            moment_copies.append(copy)

    for copy in moment_copies:
        copy.wait_recv()
    means = [moments[0, pl.ds(0, 1), :]] + [moved[d, pl.ds(0, 1), :] for d in hops]
    squares = [moments[0, pl.ds(1, 1), :]] + [moved[d, pl.ds(1, 1), :] for d in hops]
    mean_panel = sum(means) / nx
    spread = sum(squares) + rows * sum(jnp.square(m - mean_panel) for m in means)
    factor = 1.0 / jnp.sqrt(spread / total + 1e-06)
    for copy in cross_copies:
        copy.wait_recv()
    value = score[...]
    for d in hops:
        value = value + arrived[d].astype(F32)
    score[...] = value * factor

    for copy in line_copies + twin_copies + raw_copies + back_copies + moment_copies + cross_copies:
        copy.wait_send()
    for copy in (core_copy, pair_copy, back_pair, back_core, back_forward):
        copy.wait_send()

    @pl.when(gx < nx - 1)
    def _():
        halo_copy.wait_send()


def body(pressure, fir_taps, influence, mode_impulse, mode_taps):
    nx, ny, nz = (lax.axis_size(name) for name in ("gx", "gy", "gz"))
    rows, panels = pressure.shape
    total = rows * nx
    rim = fir_taps.shape[0] - 1
    modes = influence.shape[0]
    own = modes // (nx * ny * nz)
    own_panels = panels // nx
    dyn = mode_impulse.shape[1]
    fits = own % 16 == 0 and lax.axis_size("wind") == 2 and modes % 32 == 0 and ny == nz == 2 and rows % SPAN == 0 and own_panels % COLS == 0
    if not fits or rim % LEAD or dyn > LEAD:
        return plain_body(pressure, fir_taps, influence, mode_impulse, mode_taps)

    first_mode = lax.axis_index(("gx", "gy", "gz")) * own
    own_impulse = lax.dynamic_slice_in_dim(mode_impulse, first_mode, own, 0)
    own_limits = lax.dynamic_slice_in_dim(mode_taps, first_mode, own, 0)
    kept = jnp.arange(dyn, dtype=jnp.int32)[None, :] < own_limits[:, None]
    gains = jnp.where(kept, own_impulse, 0.0)
    width = SPAN + rim
    tap_rows = jnp.broadcast_to(jnp.pad(fir_taps, (0, width - rim - 1))[None], (16, width))

    vmem = pl.BlockSpec(memory_space=pltpu.VMEM)
    responses, scores = pl.pallas_call(
        functools.partial(tower_kernel, nx, own, dyn),
        out_shape=(
            jax.ShapeDtypeStruct((own, total), BF16),
            jax.ShapeDtypeStruct((modes, own_panels), F32),
        ),
        in_specs=[vmem, pl.BlockSpec(memory_space=pl.ANY), vmem, vmem],
        out_specs=(vmem, vmem),
        scratch_shapes=[
            pltpu.VMEM((rows, panels), BF16),
            pltpu.SemaphoreType.DMA,
            pltpu.VMEM((nx, modes, own_panels), BF16),
            pltpu.VMEM((nx, 2, 2, own, rows), F32),
            pltpu.VMEM((nx, 2, own, rows), F32),
            pltpu.VMEM((nx, 2, own, rows), F32),
            pltpu.VMEM((nx, own, rows), F32),
            pltpu.VMEM((nx, own, rows), F32),
            pltpu.VMEM((nx, own, rows), F32),
            pltpu.VMEM((own, rim + total), F32),
            pltpu.VMEM((own, LEAD + total), F32),
            pltpu.VMEM((dyn, own, LEAD), F32),
            pltpu.VMEM((own, total + rim), BF16),
            pltpu.VMEM((SPAN, width), BF16),
            pltpu.VMEM((SPAN, width), BF16),
            pltpu.VMEM((rim, panels), BF16),
            pltpu.VMEM((rows, panels), BF16),
            pltpu.VMEM((nx, own, rows), BF16),
            pltpu.VMEM((nx, 2, 2, own, rows), BF16),
            pltpu.VMEM((nx, modes, own_panels), BF16),
            pltpu.VMEM((nx, modes, own_panels), BF16),
            pltpu.VMEM((nx, 8, own_panels), F32),
            pltpu.VMEM((nx, 8, own_panels), F32),
            pltpu.SemaphoreType.DMA((6 * nx + 6,)),
            pltpu.SemaphoreType.DMA((6 * nx + 6,)),
        ],
        compiler_params=pltpu.CompilerParams(
            collective_id=0, has_side_effects=True, vmem_limit_bytes=48 * 1024 * 1024
        ),
    )(influence.reshape(modes, own_panels), pressure, tap_rows, gains)
    return responses, scores.reshape(influence.shape)


def solution(mesh):
    return jax.shard_map(
        body,
        mesh=mesh,
        in_specs=(
            P(("wind", "gx"), ("gy", "gz")),
            P(),
            P(None, ("gy", "gz"), "gx", None),
            P(),
            P(),
        ),
        out_specs=(P(("wind", "gx", "gy", "gz"), None), P("wind", ("gy", "gz"), "gx", None)),
        check_vma=False,
    )
```

```python
import functools
import math

import jax
import jax.numpy as jnp
from jax import lax
from jax.experimental import pallas as pl
from jax.experimental.pallas import tpu as pltpu
from jax.sharding import PartitionSpec as P

F32 = jnp.float32
BF16 = jnp.bfloat16


def dot(a, b, contract):
    return lax.dot_general(a, b, (contract, ((), ())), preferred_element_type=F32)


def band_matrix(tap_row, row_count):
    tap_count = tap_row.shape[0]
    extended = jnp.concatenate([tap_row, jnp.zeros((row_count,), tap_row.dtype)])
    flat = jnp.tile(extended, row_count)[: row_count * (row_count + tap_count - 1)]
    return flat.reshape(row_count, row_count + tap_count - 1)


def windows(padded, block, width):
    count = (padded.shape[1] - (width - block)) // block
    return jnp.stack([padded[:, i * block : i * block + width] for i in range(count)], axis=1)


def dynamic_filter(series, impulse, tap_limits):
    impulse_len = impulse.shape[1]
    kept_mask = jnp.arange(impulse_len, dtype=jnp.int32)[None, :] < tap_limits[:, None]
    kernel_taps = jnp.where(kept_mask, impulse, jnp.zeros_like(impulse))[:, ::-1]
    result = lax.conv_general_dilated(
        series[None],
        kernel_taps[:, None, :],
        window_strides=(1,),
        padding=[(impulse_len - 1, 0)],
        dimension_numbers=("NCH", "OIH", "NCH"),
        feature_group_count=series.shape[0],
        precision=lax.Precision.HIGHEST,
    )
    return result[0]


def panel_moments(pressure, halo, band, block):
    rows = pressure.shape[0]
    padded = jnp.concatenate([halo, pressure], axis=0)
    width = band.shape[1]
    parts = [
        dot(band, padded[o : o + width], ((1,), (0,))) for o in range(0, rows, block)
    ]
    filtered = jnp.concatenate(parts, axis=0).astype(BF16)
    wide = filtered.astype(F32)
    mean = jnp.mean(wide, axis=0)
    spread = jnp.sum(jnp.square(wide - mean[None, :]), axis=0)
    return mean, spread


def plain_body(pressure, fir_taps, influence, mode_impulse, mode_taps):
    nx, ng = lax.axis_size("gx"), lax.axis_size(("gy", "gz"))
    rows, panels = pressure.shape
    total = rows * nx
    rim = fir_taps.shape[0] - 1
    modes = influence.shape[0]
    own = modes // (nx * ng)
    own_panels = panels // nx
    block = min(512, rows)

    lines = lax.all_gather(influence.reshape(modes, -1), "gx", axis=1, tiled=True)
    halo = lax.ppermute(pressure[rows - rim :], "gx", [(i, i + 1) for i in range(nx - 1)])

    raw = dot(lines, pressure, ((1,), (1,)))
    raw = lax.psum_scatter(
        raw.reshape(nx, ng * own, rows), ("gy", "gz"), scatter_dimension=1, tiled=True
    )
    raw = lax.all_to_all(raw, "gx", split_axis=0, concat_axis=0, tiled=True)
    raw = raw.transpose(1, 0, 2).reshape(own, total)

    forward = band_matrix(fir_taps, 512)
    backward = band_matrix(fir_taps[::-1], 512)
    width = forward.shape[1]
    padded = jnp.pad(raw, ((0, 0), (rim, 0)))
    high = padded.astype(BF16)
    low = (padded - high.astype(F32)).astype(BF16)
    loads = sum(
        dot(windows(x, 512, width).reshape(-1, width), backward, ((1,), (1,)))
        for x in (high, low)
    ).reshape(own, total)

    first_mode = lax.axis_index(("gx", "gy", "gz")) * own
    own_impulse = lax.dynamic_slice_in_dim(mode_impulse, first_mode, own, 0)
    own_limits = lax.dynamic_slice_in_dim(mode_taps, first_mode, own, 0)
    responses = dynamic_filter(loads, own_impulse, own_limits).astype(BF16)

    resp_wide = responses.astype(F32)
    mean_mode = jnp.mean(resp_wide, axis=1)
    spread_mode = jnp.sqrt(jnp.mean(jnp.square(resp_wide - mean_mode[:, None]), axis=1) + 1e-06)
    ahead = windows(jnp.pad(responses, ((0, 0), (0, rim))), 512, width).reshape(-1, width)
    back = dot(ahead, forward, ((1,), (1,))).reshape(own, total)
    left = total - 1 - jnp.arange(total, dtype=jnp.int32)
    within = jnp.arange(rim + 1, dtype=jnp.int32)[:, None] <= left[None, :]
    reach = jnp.sum(jnp.where(within, fir_taps.astype(F32)[:, None], 0.0), axis=0)
    scale = 1.0 / (math.sqrt(total) * spread_mode)
    back = ((back - mean_mode[:, None] * reach[None, :]) * scale[:, None]).astype(BF16)

    back = back.reshape(own, nx, rows).transpose(1, 0, 2)
    back = lax.all_to_all(back, "gx", split_axis=0, concat_axis=0, tiled=True)
    back = lax.all_gather(back, ("gy", "gz"), axis=1, tiled=True).reshape(modes, rows)

    cross = dot(back, pressure, ((1,), (0,))).astype(BF16)
    cross = lax.all_to_all(
        cross.reshape(modes, nx, own_panels), "gx", split_axis=1, concat_axis=1, tiled=True
    )
    cross = jnp.sum(cross.astype(F32), axis=1)

    mean_part, square_part = panel_moments(
        pressure, halo, band_matrix(fir_taps[::-1], block), block
    )
    moments = jnp.stack([mean_part, square_part]).reshape(2, nx, own_panels)
    moments = lax.all_to_all(moments, "gx", split_axis=1, concat_axis=1, tiled=True)
    mean_panel = jnp.mean(moments[0], axis=0)
    squares = jnp.sum(
        moments[1] + rows * jnp.square(moments[0] - mean_panel[None, :]), axis=0
    )
    spread_panel = jnp.sqrt(squares / total + 1e-06)
    scores = cross / spread_panel[None, :]
    return (responses, scores.reshape(influence.shape))


SPAN = 512
LEAD = 128
COLS = 256


def tower_kernel(
    nx, own, dyn, infl, outside, taps, gains, resp, score, press, fetched,
    lines, raw, from_core, core_sum, from_pair, pair_sum, slots, series, loads, wide_gain,
    modal, band_back, band_fwd, before, after, tail, filt, turned, back, part, arrived, moments, moved,
    send, recv,
):
    rows, panels = press.shape
    modes, own_panels = infl.shape
    total = rows * nx
    rim = before.shape[0]
    half = panels // 2
    strip = rim // 2
    spans = total // SPAN
    wind = lax.axis_index("wind")
    gx, gy, gz = lax.axis_index("gx"), lax.axis_index("gy"), lax.axis_index("gz")
    mesh_id = pl.DeviceIdType.MESH

    def remote(src, dst, sem, device):
        return pltpu.make_async_remote_copy(
            src_ref=src, dst_ref=dst, send_sem=send.at[sem], recv_sem=recv.at[sem],
            device_id=device, device_id_type=mesh_id,
        )

    def ahead(d):
        return lax.rem(gx + d, nx)

    def behind(d):
        return lax.rem(gx + nx - d, nx)

    def columns(index, size):
        return pl.ds(pl.multiple_of(index * size, size), size)

    hops = range(1, nx)
    first = {name: i * nx for i, name in enumerate(("lines", "raw", "back", "cross", "moments", "twin"))}
    extra = 6 * nx

    fetch = pltpu.make_async_copy(outside, press, fetched)
    fetch.start()
    barrier = pltpu.get_barrier_semaphore()
    peers = [{"gx": ahead(d)} for d in hops] + [{"gy": 1 - gy}, {"gz": 1 - gz}, {"wind": 1 - wind}]
    for peer in peers:
        pl.semaphore_signal(barrier, inc=1, device_id=peer, device_id_type=mesh_id)
    pl.semaphore_wait(barrier, len(peers))

    share = columns(wind, modes // 2)
    line_copies = [
        remote(infl.at[share], lines.at[d, share], first["lines"] + d, {"gx": ahead(d)})
        for d in hops
    ]
    twin_copies = [
        remote(lines.at[d, share], lines.at[d, share], first["twin"] + d, {"wind": 1 - wind})
        for d in hops
    ]
    for copy in line_copies:
        copy.start()
    up_copies = [
        remote(
            press.at[pl.ds(rows - rim + k * strip, strip), pl.ds(0, half)],
            before.at[pl.ds(k * strip, strip)], extra + 6 + k, {"gx": ahead(1)},
        )
        for k in range(2)
    ]
    down_copies = [
        remote(
            press.at[pl.ds(k * strip, strip), pl.ds(half, half)],
            after.at[pl.ds(k * strip, strip)], extra + 8 + k, {"gx": behind(1)},
        )
        for k in range(2)
    ]

    def start_strips(k):
        @pl.when(gx < nx - 1)
        def _():
            up_copies[k].start()

        @pl.when(gx > 0)
        def _():
            down_copies[k].start()

    width = band_back.shape[1]
    reach_to = rim + LEAD
    cross_sum = lax.broadcasted_iota(jnp.int32, (reach_to, reach_to), 0)
    cross_sum += lax.broadcasted_iota(jnp.int32, (reach_to, reach_to), 1)
    flip = jnp.where(cross_sum == rim, 1.0, 0.0).astype(BF16)
    reverse = dot(taps[:, pl.ds(0, reach_to)], flip, ((1,), (0,)))[0:1]
    reverse = jnp.concatenate([reverse, jnp.zeros((1, width - reach_to), F32)], axis=1)
    tap_line = taps[...].astype(F32)[0:1]
    for c in range(SPAN // LEAD):
        for tap_row, band in ((tap_line, band_fwd), (reverse, band_back)):
            line = jnp.broadcast_to(tap_row, (LEAD, width))
            band[pl.ds(c * LEAD, LEAD), :] = pltpu.roll(
                line, c * LEAD, 1, stride=1, stride_axis=0
            ).astype(BF16)
    for k in range(dyn):
        wide_gain[k] = jnp.broadcast_to(gains[:, k : k + 1], (own, LEAD))
    series[:, pl.ds(0, rim)] = jnp.zeros((own, rim), F32)
    loads[:, pl.ds(0, LEAD)] = jnp.zeros((own, LEAD), F32)
    modal[:, pl.ds(total, rim)] = jnp.zeros((own, rim), BF16)
    moments[...] = jnp.zeros(moments.shape, F32)

    @pl.when(gx == 0)
    def _():
        before[...] = jnp.zeros(before.shape, BF16)

    @pl.when(gx == nx - 1)
    def _():
        after[...] = jnp.zeros(after.shape, BF16)

    def add_lines(block, held, fresh):
        def step(i, _):
            at = columns(i, COLS)
            piece = press[at, columns(block, own_panels)]
            term = dot(held[...], piece, ((1,), (1,))).reshape(nx, 2, 2, own, COLS)
            if fresh:
                raw[:, :, :, :, at] = term
            else:
                raw[:, :, :, :, at] += term
            return 0

        lax.fori_loop(0, rows // COLS, step, 0)

    fetch.wait()
    add_lines(gx, infl, True)

    def filter_later(i, _):
        at = columns(i, COLS)
        for o in range(SPAN, rows, SPAN):
            piece = press[pl.ds(o - rim, SPAN + rim), at]
            filt[pl.ds(o, SPAN), at] = dot(band_back[...], piece, ((1,), (0,))).astype(BF16)
        own_part = dot(band_back[:, pl.ds(rim, SPAN)], press[pl.ds(0, SPAN), at], ((1,), (0,)))
        filt[pl.ds(0, SPAN), at] = own_part.astype(BF16)
        return 0

    lax.fori_loop(0, panels // COLS, filter_later, 0)

    order = sorted(hops, key=lambda d: min(d, nx - d))
    for d in order:
        line_copies[d - 1].wait_recv()
        twin_copies[d - 1].start()
    for d in order:
        twin_copies[d - 1].wait_recv()
        add_lines(behind(d), lines.at[d], False)

    start_strips(0)

    core_copy = remote(raw.at[:, :, 1 - gz], from_core, extra + 1, {"gz": 1 - gz})
    core_copy.start()
    core_copy.wait_recv()
    core_sum[...] = raw[:, :, gz] + from_core[...]
    pair_copy = remote(core_sum.at[:, 1 - gy], from_pair, extra + 2, {"gy": 1 - gy})
    pair_copy.start()
    pair_copy.wait_recv()
    pair_sum[...] = core_sum[:, gy] + from_pair[...]
    raw_copies = [
        remote(pair_sum.at[ahead(d)], slots.at[d], first["raw"] + d, {"gx": ahead(d)})
        for d in hops
    ]
    for copy in raw_copies:
        copy.start()

    def place(block):
        return pl.ds(pl.multiple_of(block * rows + rim, LEAD), rows)

    series[:, place(gx)] = pair_sum[gx]
    for d, copy in zip(hops, raw_copies):
        copy.wait_recv()
        series[:, place(behind(d))] = slots[d]
    start_strips(1)

    high, low = [], []
    for i in range(spans):
        piece = series[:, pl.ds(i * SPAN, SPAN + rim)]
        top = piece.astype(BF16)
        high.append(top)
        low.append((piece - top.astype(F32)).astype(BF16))
    both = dot(jnp.concatenate(high + low, axis=0), band_back[...], ((1,), (1,)))
    for i in range(spans):
        loads[:, pl.ds(LEAD + i * SPAN, SPAN)] = (
            both[i * own : (i + 1) * own] + both[(spans + i) * own : (spans + i + 1) * own]
        )

    def respond(i, _):
        piece = loads[:, pl.ds(pl.multiple_of(i * SPAN, SPAN), SPAN + LEAD)]
        result = jnp.zeros((own, SPAN), F32)
        for k in range(dyn):
            gain = jnp.concatenate([wide_gain[k]] * (SPAN // LEAD), axis=1)
            moved_by = piece if k == 0 else pltpu.roll(piece, k, 1)
            result = result + gain * moved_by[:, LEAD:]
        modal[:, columns(i, SPAN)] = result.astype(BF16)
        return 0

    lax.fori_loop(0, spans, respond, 0)

    settled = modal[:, pl.ds(0, total)]
    resp[...] = settled
    wide = settled.astype(F32)
    mean_mode = jnp.mean(wide, axis=1, keepdims=True)
    off = wide - mean_mode
    spread_mode = jnp.sqrt(jnp.mean(off * off, axis=1, keepdims=True) + 1e-06)
    scale = 1.0 / (math.sqrt(total) * spread_mode)

    later = [modal[:, pl.ds(i * SPAN, SPAN + rim)] for i in range(spans)]
    lane = lax.broadcasted_iota(jnp.int32, (own, width), 1)
    full = jnp.ones((own, width), F32).astype(BF16)
    cut = jnp.where(lane < SPAN, 1.0, 0.0).astype(BF16)
    turned_wide = dot(jnp.concatenate(later + [full, cut], axis=0), band_fwd[...], ((1,), (1,)))
    reach = [turned_wide[(spans + j) * own : (spans + j + 1) * own] for j in range(2)]
    for i in range(spans):
        value = turned_wide[i * own : (i + 1) * own] - mean_mode * reach[int(i == spans - 1)]
        block, offset = divmod(i * SPAN, rows)
        turned[block, :, pl.ds(offset, SPAN)] = (value * scale).astype(BF16)

    back_copies = [
        remote(turned.at[ahead(d)], back.at[gx, gy, gz], first["back"] + d, {"gx": ahead(d)})
        for d in hops
    ]
    for copy in back_copies:
        copy.start()
    back[gx, gy, gz] = turned[gx]

    for copy in back_copies:
        copy.wait_recv()
    mine = back.at[:, gy, gz]
    back_pair = remote(mine, mine, extra + 3, {"gy": 1 - gy})
    back_core = remote(mine, mine, extra + 4, {"gz": 1 - gz})
    back_pair.start()
    back_core.start()
    back_pair.wait_recv()
    other = back.at[:, 1 - gy, gz]
    back_forward = remote(other, other, extra + 5, {"gz": 1 - gz})
    back_forward.start()
    back_core.wait_recv()
    back_forward.wait_recv()

    def cross_block(block, j):
        at = pl.ds(pl.multiple_of(block * own_panels + j * COLS, COLS), COLS)
        return dot(back[...].reshape(modes, rows), press[:, at], ((1,), (0,)))

    cross_copies = []
    for d in hops:
        for j in range(own_panels // COLS):
            part[d, :, pl.ds(j * COLS, COLS)] = cross_block(ahead(d), j).astype(BF16)
        copy = remote(part.at[d], arrived.at[d], first["cross"] + d, {"gx": ahead(d)})
        copy.start()
        cross_copies.append(copy)
    for j in range(own_panels // COLS):
        score[:, pl.ds(j * COLS, COLS)] = cross_block(gx, j)

    @pl.when(gx > 0)
    def _():
        for copy in up_copies:
            copy.wait_recv()

    @pl.when(gx < nx - 1)
    def _():
        for copy in down_copies:
            copy.wait_recv()

    def filter_first(i, _):
        at = columns(i, COLS)
        far = pl.ds(pl.multiple_of(half + i * COLS, COLS), COLS)
        older = band_back[pl.ds(0, rim), pl.ds(0, rim)]
        newer = band_back[pl.ds(0, rim), pl.ds(rim, rim)]
        value = dot(older, before[:, at], ((1,), (0,)))
        value += dot(newer, press[pl.ds(0, rim), at], ((1,), (0,)))
        filt[pl.ds(0, rim), at] = value.astype(BF16)
        value = dot(older, press[pl.ds(rows - rim, rim), far], ((1,), (0,)))
        value += dot(newer, after[:, at], ((1,), (0,)))
        tail[:, at] = value.astype(BF16)
        return 0

    def measure(block, slot):
        upper = block >= nx // 2
        with_first = jnp.where(jnp.logical_or(block < nx // 2, gx == 0), 1.0, 0.0)
        with_tail = jnp.where(jnp.logical_and(upper, gx < nx - 1), 1.0, 0.0)
        count = rows - rim + rim * (with_first + with_tail)
        for j in range(own_panels // COLS):
            at = pl.ds(pl.multiple_of(block * own_panels + j * COLS, COLS), COLS)
            begin = lax.rem(block, nx // 2) * own_panels + j * COLS
            pieces = (
                (1.0, filt[pl.ds(rim, rows - rim), at].astype(F32)),
                (with_first, filt[pl.ds(0, rim), at].astype(F32)),
                (with_tail, tail[:, pl.ds(pl.multiple_of(begin, COLS), COLS)].astype(F32)),
            )
            mean = sum(w * jnp.sum(v, axis=0, keepdims=True) for w, v in pieces) / count
            moments[slot, pl.ds(0, 1), pl.ds(j * COLS, COLS)] = mean
            moments[slot, pl.ds(1, 1), pl.ds(j * COLS, COLS)] = sum(
                w * jnp.sum(jnp.square(v - mean), axis=0, keepdims=True) for w, v in pieces
            )

    lax.fori_loop(0, half // COLS, filter_first, 0)
    moment_copies = []
    for d in range(nx):
        measure(ahead(d), d)
        if d:
            copy = remote(moments.at[d], moved.at[d], first["moments"] + d, {"gx": ahead(d)})
            copy.start()
            moment_copies.append(copy)

    for copy in moment_copies:
        copy.wait_recv()
    means = [moments[0, pl.ds(0, 1), :]] + [moved[d, pl.ds(0, 1), :] for d in hops]
    squares = [moments[0, pl.ds(1, 1), :]] + [moved[d, pl.ds(1, 1), :] for d in hops]
    uneven = jnp.where(gx >= nx // 2, 1.0 * rim, 0.0)
    counts = []
    for d in range(nx):
        source = behind(d)
        sign = jnp.where(source == 0, 1.0, 0.0) - jnp.where(source == nx - 1, 1.0, 0.0)
        counts.append(rows + uneven * sign)
    mean_panel = sum(n * m for n, m in zip(counts, means)) / total
    spread = sum(squares) + sum(n * jnp.square(m - mean_panel) for n, m in zip(counts, means))
    factor = 1.0 / jnp.sqrt(spread / total + 1e-06)
    for copy in cross_copies:
        copy.wait_recv()
    value = score[...]
    for d in hops:
        value = value + arrived[d].astype(F32)
    score[...] = value * factor

    for copy in line_copies + twin_copies + raw_copies + back_copies + moment_copies + cross_copies:
        copy.wait_send()
    for copy in (core_copy, pair_copy, back_pair, back_core, back_forward):
        copy.wait_send()

    @pl.when(gx < nx - 1)
    def _():
        for copy in up_copies:
            copy.wait_send()

    @pl.when(gx > 0)
    def _():
        for copy in down_copies:
            copy.wait_send()


def body(pressure, fir_taps, influence, mode_impulse, mode_taps):
    nx, ny, nz = (lax.axis_size(name) for name in ("gx", "gy", "gz"))
    rows, panels = pressure.shape
    total = rows * nx
    rim = fir_taps.shape[0] - 1
    modes = influence.shape[0]
    own = modes // (nx * ny * nz)
    own_panels = panels // nx
    dyn = mode_impulse.shape[1]
    fits = own % 16 == 0 and lax.axis_size("wind") == 2 and modes % 32 == 0 and ny == nz == 2 and rows % SPAN == 0 and own_panels % COLS == 0 and nx % 2 == 0
    if not fits or rim % LEAD or dyn > LEAD:
        return plain_body(pressure, fir_taps, influence, mode_impulse, mode_taps)

    first_mode = lax.axis_index(("gx", "gy", "gz")) * own
    own_impulse = lax.dynamic_slice_in_dim(mode_impulse, first_mode, own, 0)
    own_limits = lax.dynamic_slice_in_dim(mode_taps, first_mode, own, 0)
    kept = jnp.arange(dyn, dtype=jnp.int32)[None, :] < own_limits[:, None]
    gains = jnp.where(kept, own_impulse, 0.0)
    width = SPAN + rim
    tap_rows = jnp.broadcast_to(jnp.pad(fir_taps, (0, width - rim - 1))[None], (16, width))

    vmem = pl.BlockSpec(memory_space=pltpu.VMEM)
    responses, scores = pl.pallas_call(
        functools.partial(tower_kernel, nx, own, dyn),
        out_shape=(
            jax.ShapeDtypeStruct((own, total), BF16),
            jax.ShapeDtypeStruct((modes, own_panels), F32),
        ),
        in_specs=[vmem, pl.BlockSpec(memory_space=pl.ANY), vmem, vmem],
        out_specs=(vmem, vmem),
        scratch_shapes=[
            pltpu.VMEM((rows, panels), BF16),
            pltpu.SemaphoreType.DMA,
            pltpu.VMEM((nx, modes, own_panels), BF16),
            pltpu.VMEM((nx, 2, 2, own, rows), F32),
            pltpu.VMEM((nx, 2, own, rows), F32),
            pltpu.VMEM((nx, 2, own, rows), F32),
            pltpu.VMEM((nx, own, rows), F32),
            pltpu.VMEM((nx, own, rows), F32),
            pltpu.VMEM((nx, own, rows), F32),
            pltpu.VMEM((own, rim + total), F32),
            pltpu.VMEM((own, LEAD + total), F32),
            pltpu.VMEM((dyn, own, LEAD), F32),
            pltpu.VMEM((own, total + rim), BF16),
            pltpu.VMEM((SPAN, width), BF16),
            pltpu.VMEM((SPAN, width), BF16),
            pltpu.VMEM((rim, panels // 2), BF16),
            pltpu.VMEM((rim, panels // 2), BF16),
            pltpu.VMEM((rim, panels // 2), BF16),
            pltpu.VMEM((rows, panels), BF16),
            pltpu.VMEM((nx, own, rows), BF16),
            pltpu.VMEM((nx, 2, 2, own, rows), BF16),
            pltpu.VMEM((nx, modes, own_panels), BF16),
            pltpu.VMEM((nx, modes, own_panels), BF16),
            pltpu.VMEM((nx, 8, own_panels), F32),
            pltpu.VMEM((nx, 8, own_panels), F32),
            pltpu.SemaphoreType.DMA((6 * nx + 10,)),
            pltpu.SemaphoreType.DMA((6 * nx + 10,)),
        ],
        compiler_params=pltpu.CompilerParams(
            collective_id=0, has_side_effects=True, vmem_limit_bytes=48 * 1024 * 1024
        ),
    )(influence.reshape(modes, own_panels), pressure, tap_rows, gains)
    return responses, scores.reshape(influence.shape)


def solution(mesh):
    return jax.shard_map(
        body,
        mesh=mesh,
        in_specs=(
            P(("wind", "gx"), ("gy", "gz")),
            P(),
            P(None, ("gy", "gz"), "gx", None),
            P(),
            P(),
        ),
        out_specs=(P(("wind", "gx", "gy", "gz"), None), P("wind", ("gy", "gz"), "gx", None)),
        check_vma=False,
    )
```

```python
import functools
import math

import jax
import jax.numpy as jnp
from jax import lax
from jax.experimental import pallas as pl
from jax.experimental.pallas import tpu as pltpu
from jax.sharding import PartitionSpec as P

F32 = jnp.float32
BF16 = jnp.bfloat16


def dot(a, b, contract):
    return lax.dot_general(a, b, (contract, ((), ())), preferred_element_type=F32)


def band_matrix(tap_row, row_count):
    tap_count = tap_row.shape[0]
    extended = jnp.concatenate([tap_row, jnp.zeros((row_count,), tap_row.dtype)])
    flat = jnp.tile(extended, row_count)[: row_count * (row_count + tap_count - 1)]
    return flat.reshape(row_count, row_count + tap_count - 1)


def windows(padded, block, width):
    count = (padded.shape[1] - (width - block)) // block
    return jnp.stack([padded[:, i * block : i * block + width] for i in range(count)], axis=1)


def dynamic_filter(series, impulse, tap_limits):
    impulse_len = impulse.shape[1]
    kept_mask = jnp.arange(impulse_len, dtype=jnp.int32)[None, :] < tap_limits[:, None]
    kernel_taps = jnp.where(kept_mask, impulse, jnp.zeros_like(impulse))[:, ::-1]
    result = lax.conv_general_dilated(
        series[None],
        kernel_taps[:, None, :],
        window_strides=(1,),
        padding=[(impulse_len - 1, 0)],
        dimension_numbers=("NCH", "OIH", "NCH"),
        feature_group_count=series.shape[0],
        precision=lax.Precision.HIGHEST,
    )
    return result[0]


def panel_moments(pressure, halo, band, block):
    rows = pressure.shape[0]
    padded = jnp.concatenate([halo, pressure], axis=0)
    width = band.shape[1]
    parts = [
        dot(band, padded[o : o + width], ((1,), (0,))) for o in range(0, rows, block)
    ]
    filtered = jnp.concatenate(parts, axis=0).astype(BF16)
    wide = filtered.astype(F32)
    mean = jnp.mean(wide, axis=0)
    spread = jnp.sum(jnp.square(wide - mean[None, :]), axis=0)
    return mean, spread


def plain_body(pressure, fir_taps, influence, mode_impulse, mode_taps):
    nx, ng = lax.axis_size("gx"), lax.axis_size(("gy", "gz"))
    rows, panels = pressure.shape
    total = rows * nx
    rim = fir_taps.shape[0] - 1
    modes = influence.shape[0]
    own = modes // (nx * ng)
    own_panels = panels // nx
    block = min(512, rows)

    lines = lax.all_gather(influence.reshape(modes, -1), "gx", axis=1, tiled=True)
    halo = lax.ppermute(pressure[rows - rim :], "gx", [(i, i + 1) for i in range(nx - 1)])

    raw = dot(lines, pressure, ((1,), (1,)))
    raw = lax.psum_scatter(
        raw.reshape(nx, ng * own, rows), ("gy", "gz"), scatter_dimension=1, tiled=True
    )
    raw = lax.all_to_all(raw, "gx", split_axis=0, concat_axis=0, tiled=True)
    raw = raw.transpose(1, 0, 2).reshape(own, total)

    forward = band_matrix(fir_taps, 512)
    backward = band_matrix(fir_taps[::-1], 512)
    width = forward.shape[1]
    padded = jnp.pad(raw, ((0, 0), (rim, 0)))
    high = padded.astype(BF16)
    low = (padded - high.astype(F32)).astype(BF16)
    loads = sum(
        dot(windows(x, 512, width).reshape(-1, width), backward, ((1,), (1,)))
        for x in (high, low)
    ).reshape(own, total)

    first_mode = lax.axis_index(("gx", "gy", "gz")) * own
    own_impulse = lax.dynamic_slice_in_dim(mode_impulse, first_mode, own, 0)
    own_limits = lax.dynamic_slice_in_dim(mode_taps, first_mode, own, 0)
    responses = dynamic_filter(loads, own_impulse, own_limits).astype(BF16)

    resp_wide = responses.astype(F32)
    mean_mode = jnp.mean(resp_wide, axis=1)
    spread_mode = jnp.sqrt(jnp.mean(jnp.square(resp_wide - mean_mode[:, None]), axis=1) + 1e-06)
    ahead = windows(jnp.pad(responses, ((0, 0), (0, rim))), 512, width).reshape(-1, width)
    back = dot(ahead, forward, ((1,), (1,))).reshape(own, total)
    left = total - 1 - jnp.arange(total, dtype=jnp.int32)
    within = jnp.arange(rim + 1, dtype=jnp.int32)[:, None] <= left[None, :]
    reach = jnp.sum(jnp.where(within, fir_taps.astype(F32)[:, None], 0.0), axis=0)
    scale = 1.0 / (math.sqrt(total) * spread_mode)
    back = ((back - mean_mode[:, None] * reach[None, :]) * scale[:, None]).astype(BF16)

    back = back.reshape(own, nx, rows).transpose(1, 0, 2)
    back = lax.all_to_all(back, "gx", split_axis=0, concat_axis=0, tiled=True)
    back = lax.all_gather(back, ("gy", "gz"), axis=1, tiled=True).reshape(modes, rows)

    cross = dot(back, pressure, ((1,), (0,))).astype(BF16)
    cross = lax.all_to_all(
        cross.reshape(modes, nx, own_panels), "gx", split_axis=1, concat_axis=1, tiled=True
    )
    cross = jnp.sum(cross.astype(F32), axis=1)

    mean_part, square_part = panel_moments(
        pressure, halo, band_matrix(fir_taps[::-1], block), block
    )
    moments = jnp.stack([mean_part, square_part]).reshape(2, nx, own_panels)
    moments = lax.all_to_all(moments, "gx", split_axis=1, concat_axis=1, tiled=True)
    mean_panel = jnp.mean(moments[0], axis=0)
    squares = jnp.sum(
        moments[1] + rows * jnp.square(moments[0] - mean_panel[None, :]), axis=0
    )
    spread_panel = jnp.sqrt(squares / total + 1e-06)
    scores = cross / spread_panel[None, :]
    return (responses, scores.reshape(influence.shape))


SPAN = 512
LEAD = 128
COLS = 256


def tower_kernel(
    nx, own, dyn, infl, outside, taps, gains, resp, score, press, fetched,
    lines, raw, from_core, core_sum, from_pair, pair_sum, slots, series, loads, wide_gain,
    modal, band_back, band_fwd, before, after, tail, filt, turned, back, part, arrived, moments, moved,
    send, recv,
):
    rows, panels = press.shape
    modes, own_panels = infl.shape
    total = rows * nx
    rim = before.shape[0]
    half = panels // 2
    strip = rim // 2
    spans = total // SPAN
    wind = lax.axis_index("wind")
    gx, gy, gz = lax.axis_index("gx"), lax.axis_index("gy"), lax.axis_index("gz")
    mesh_id = pl.DeviceIdType.MESH

    def remote(src, dst, sem, device):
        return pltpu.make_async_remote_copy(
            src_ref=src, dst_ref=dst, send_sem=send.at[sem], recv_sem=recv.at[sem],
            device_id=device, device_id_type=mesh_id,
        )

    def ahead(d):
        return lax.rem(gx + d, nx)

    def behind(d):
        return lax.rem(gx + nx - d, nx)

    def columns(index, size):
        return pl.ds(pl.multiple_of(index * size, size), size)

    hops = range(1, nx)
    first = {name: i * nx for i, name in enumerate(("lines", "raw", "back", "cross", "moments", "twin"))}
    extra = 6 * nx

    fetch = pltpu.make_async_copy(outside, press, fetched)
    fetch.start()
    barrier = pltpu.get_barrier_semaphore()
    peers = [{"gx": ahead(d)} for d in hops] + [{"gy": 1 - gy}, {"gz": 1 - gz}, {"wind": 1 - wind}]
    for peer in peers:
        pl.semaphore_signal(barrier, inc=1, device_id=peer, device_id_type=mesh_id)
    pl.semaphore_wait(barrier, len(peers))

    share = columns(wind, modes // 2)
    line_copies = [
        remote(infl.at[share], lines.at[d, share], first["lines"] + d, {"gx": ahead(d)})
        for d in hops
    ]
    twin_copies = [
        remote(lines.at[d, share], lines.at[d, share], first["twin"] + d, {"wind": 1 - wind})
        for d in hops
    ]
    for copy in line_copies:
        copy.start()
    up_copies = [
        remote(
            press.at[pl.ds(rows - rim + k * strip, strip), pl.ds(0, half)],
            before.at[pl.ds(k * strip, strip)], extra + 6 + k, {"gx": ahead(1)},
        )
        for k in range(2)
    ]
    down_copies = [
        remote(
            press.at[pl.ds(k * strip, strip), pl.ds(half, half)],
            after.at[pl.ds(k * strip, strip)], extra + 8 + k, {"gx": behind(1)},
        )
        for k in range(2)
    ]

    def start_strips(k):
        @pl.when(gx < nx - 1)
        def _():
            up_copies[k].start()

        @pl.when(gx > 0)
        def _():
            down_copies[k].start()

    width = band_back.shape[1]
    reach_to = rim + LEAD
    cross_sum = lax.broadcasted_iota(jnp.int32, (reach_to, reach_to), 0)
    cross_sum += lax.broadcasted_iota(jnp.int32, (reach_to, reach_to), 1)
    flip = jnp.where(cross_sum == rim, 1.0, 0.0).astype(BF16)
    reverse = dot(taps[:, pl.ds(0, reach_to)], flip, ((1,), (0,)))[0:1]
    reverse = jnp.concatenate([reverse, jnp.zeros((1, width - reach_to), F32)], axis=1)
    tap_line = taps[...].astype(F32)[0:1]
    for c in range(SPAN // LEAD):
        for tap_row, band in ((tap_line, band_fwd), (reverse, band_back)):
            line = jnp.broadcast_to(tap_row, (LEAD, width))
            band[pl.ds(c * LEAD, LEAD), :] = pltpu.roll(
                line, c * LEAD, 1, stride=1, stride_axis=0
            ).astype(BF16)
    for k in range(dyn):
        wide_gain[k] = jnp.broadcast_to(gains[:, k : k + 1], (own, LEAD))
    series[:, pl.ds(0, rim)] = jnp.zeros((own, rim), F32)
    loads[:, pl.ds(0, LEAD)] = jnp.zeros((own, LEAD), F32)
    modal[:, pl.ds(total, rim)] = jnp.zeros((own, rim), BF16)
    moments[...] = jnp.zeros(moments.shape, F32)

    @pl.when(gx == 0)
    def _():
        before[...] = jnp.zeros(before.shape, BF16)

    @pl.when(gx == nx - 1)
    def _():
        after[...] = jnp.zeros(after.shape, BF16)

    def add_lines(block, held, fresh):
        def step(i, _):
            at = columns(i, COLS)
            piece = press[at, columns(block, own_panels)]
            term = dot(held[...], piece, ((1,), (1,))).reshape(nx, 2, 2, own, COLS)
            if fresh:
                raw[:, :, :, :, at] = term
            else:
                raw[:, :, :, :, at] += term
            return 0

        lax.fori_loop(0, rows // COLS, step, 0)

    fetch.wait()
    add_lines(gx, infl, True)

    def filter_later(i, _):
        at = columns(i, COLS)
        for o in range(SPAN, rows, SPAN):
            piece = press[pl.ds(o - rim, SPAN + rim), at]
            filt[pl.ds(o, SPAN), at] = dot(band_back[...], piece, ((1,), (0,))).astype(BF16)
        own_part = dot(band_back[:, pl.ds(rim, SPAN)], press[pl.ds(0, SPAN), at], ((1,), (0,)))
        filt[pl.ds(0, SPAN), at] = own_part.astype(BF16)
        return 0

    lax.fori_loop(0, panels // COLS, filter_later, 0)

    order = sorted(hops, key=lambda d: min(d, nx - d))
    for d in order:
        line_copies[d - 1].wait_recv()
        twin_copies[d - 1].start()
    for d in order:
        twin_copies[d - 1].wait_recv()
        add_lines(behind(d), lines.at[d], False)

    start_strips(0)

    def place(block):
        return pl.ds(pl.multiple_of(block * rows + rim, LEAD), rows)

    turns = list(hops) + [0]
    core_base = extra + 10
    pair_base = core_base + nx
    core_copies = [
        remote(raw.at[ahead(d), :, 1 - gz], from_core.at[ahead(d)], core_base + d, {"gz": 1 - gz})
        for d in turns
    ]
    pair_copies = [
        remote(core_sum.at[ahead(d), 1 - gy], from_pair.at[ahead(d)], pair_base + d, {"gy": 1 - gy})
        for d in turns
    ]
    raw_copies = [
        remote(pair_sum.at[ahead(d)], slots.at[d], first["raw"] + d, {"gx": ahead(d)})
        for d in hops
    ]
    for copy in core_copies:
        copy.start()
    for i, d in enumerate(turns):
        core_copies[i].wait_recv()
        core_sum[ahead(d)] = raw[ahead(d), :, gz] + from_core[ahead(d)]
        pair_copies[i].start()
    for i, d in enumerate(turns):
        pair_copies[i].wait_recv()
        pair_sum[ahead(d)] = core_sum[ahead(d), gy] + from_pair[ahead(d)]
        if d:
            raw_copies[i].start()
    series[:, place(gx)] = pair_sum[gx]
    for d, copy in zip(hops, raw_copies):
        copy.wait_recv()
        series[:, place(behind(d))] = slots[d]
    start_strips(1)

    high, low = [], []
    for i in range(spans):
        piece = series[:, pl.ds(i * SPAN, SPAN + rim)]
        top = piece.astype(BF16)
        high.append(top)
        low.append((piece - top.astype(F32)).astype(BF16))
    both = dot(jnp.concatenate(high + low, axis=0), band_back[...], ((1,), (1,)))
    for i in range(spans):
        loads[:, pl.ds(LEAD + i * SPAN, SPAN)] = (
            both[i * own : (i + 1) * own] + both[(spans + i) * own : (spans + i + 1) * own]
        )

    def respond(i, _):
        piece = loads[:, pl.ds(pl.multiple_of(i * SPAN, SPAN), SPAN + LEAD)]
        result = jnp.zeros((own, SPAN), F32)
        for k in range(dyn):
            gain = jnp.concatenate([wide_gain[k]] * (SPAN // LEAD), axis=1)
            moved_by = piece if k == 0 else pltpu.roll(piece, k, 1)
            result = result + gain * moved_by[:, LEAD:]
        modal[:, columns(i, SPAN)] = result.astype(BF16)
        return 0

    lax.fori_loop(0, spans, respond, 0)

    settled = modal[:, pl.ds(0, total)]
    resp[...] = settled
    wide = settled.astype(F32)
    mean_mode = jnp.mean(wide, axis=1, keepdims=True)
    off = wide - mean_mode
    spread_mode = jnp.sqrt(jnp.mean(off * off, axis=1, keepdims=True) + 1e-06)
    scale = 1.0 / (math.sqrt(total) * spread_mode)

    later = [modal[:, pl.ds(i * SPAN, SPAN + rim)] for i in range(spans)]
    lane = lax.broadcasted_iota(jnp.int32, (own, width), 1)
    full = jnp.ones((own, width), F32).astype(BF16)
    cut = jnp.where(lane < SPAN, 1.0, 0.0).astype(BF16)
    turned_wide = dot(jnp.concatenate(later + [full, cut], axis=0), band_fwd[...], ((1,), (1,)))
    reach = [turned_wide[(spans + j) * own : (spans + j + 1) * own] for j in range(2)]
    for i in range(spans):
        value = turned_wide[i * own : (i + 1) * own] - mean_mode * reach[int(i == spans - 1)]
        block, offset = divmod(i * SPAN, rows)
        turned[block, :, pl.ds(offset, SPAN)] = (value * scale).astype(BF16)

    back_copies = [
        remote(turned.at[ahead(d)], back.at[gx, gy, gz], first["back"] + d, {"gx": ahead(d)})
        for d in hops
    ]
    for copy in back_copies:
        copy.start()
    back[gx, gy, gz] = turned[gx]

    to_pair, to_core, onward = [], [], []
    spread_base = pair_base + nx
    for d in range(nx):
        if d:
            back_copies[d - 1].wait_recv()
        mine = back.at[behind(d), gy, gz]
        to_pair.append(remote(mine, mine, spread_base + d, {"gy": 1 - gy}))
        to_core.append(remote(mine, mine, spread_base + nx + d, {"gz": 1 - gz}))
        to_pair[d].start()
        to_core[d].start()
    for d in range(nx):
        to_pair[d].wait_recv()
        other = back.at[behind(d), 1 - gy, gz]
        onward.append(remote(other, other, spread_base + 2 * nx + d, {"gz": 1 - gz}))
        onward[d].start()
    for copy in to_core + onward:
        copy.wait_recv()

    def cross_block(block, j):
        at = pl.ds(pl.multiple_of(block * own_panels + j * COLS, COLS), COLS)
        return dot(back[...].reshape(modes, rows), press[:, at], ((1,), (0,)))

    cross_copies = []
    for d in hops:
        for j in range(own_panels // COLS):
            part[d, :, pl.ds(j * COLS, COLS)] = cross_block(ahead(d), j).astype(BF16)
        copy = remote(part.at[d], arrived.at[d], first["cross"] + d, {"gx": ahead(d)})
        copy.start()
        cross_copies.append(copy)
    for j in range(own_panels // COLS):
        score[:, pl.ds(j * COLS, COLS)] = cross_block(gx, j)

    @pl.when(gx > 0)
    def _():
        for copy in up_copies:
            copy.wait_recv()

    @pl.when(gx < nx - 1)
    def _():
        for copy in down_copies:
            copy.wait_recv()

    def filter_first(i, _):
        at = columns(i, COLS)
        far = pl.ds(pl.multiple_of(half + i * COLS, COLS), COLS)
        older = band_back[pl.ds(0, rim), pl.ds(0, rim)]
        newer = band_back[pl.ds(0, rim), pl.ds(rim, rim)]
        value = dot(older, before[:, at], ((1,), (0,)))
        value += dot(newer, press[pl.ds(0, rim), at], ((1,), (0,)))
        filt[pl.ds(0, rim), at] = value.astype(BF16)
        value = dot(older, press[pl.ds(rows - rim, rim), far], ((1,), (0,)))
        value += dot(newer, after[:, at], ((1,), (0,)))
        tail[:, at] = value.astype(BF16)
        return 0

    def measure(block, slot):
        upper = block >= nx // 2
        with_first = jnp.where(jnp.logical_or(block < nx // 2, gx == 0), 1.0, 0.0)
        with_tail = jnp.where(jnp.logical_and(upper, gx < nx - 1), 1.0, 0.0)
        count = rows - rim + rim * (with_first + with_tail)
        for j in range(own_panels // COLS):
            at = pl.ds(pl.multiple_of(block * own_panels + j * COLS, COLS), COLS)
            begin = lax.rem(block, nx // 2) * own_panels + j * COLS
            pieces = (
                (1.0, filt[pl.ds(rim, rows - rim), at].astype(F32)),
                (with_first, filt[pl.ds(0, rim), at].astype(F32)),
                (with_tail, tail[:, pl.ds(pl.multiple_of(begin, COLS), COLS)].astype(F32)),
            )
            mean = sum(w * jnp.sum(v, axis=0, keepdims=True) for w, v in pieces) / count
            moments[slot, pl.ds(0, 1), pl.ds(j * COLS, COLS)] = mean
            moments[slot, pl.ds(1, 1), pl.ds(j * COLS, COLS)] = sum(
                w * jnp.sum(jnp.square(v - mean), axis=0, keepdims=True) for w, v in pieces
            )

    lax.fori_loop(0, half // COLS, filter_first, 0)
    moment_copies = []
    for d in range(nx):
        measure(ahead(d), d)
        if d:
            copy = remote(moments.at[d], moved.at[d], first["moments"] + d, {"gx": ahead(d)})
            copy.start()
            moment_copies.append(copy)

    for copy in moment_copies:
        copy.wait_recv()
    means = [moments[0, pl.ds(0, 1), :]] + [moved[d, pl.ds(0, 1), :] for d in hops]
    squares = [moments[0, pl.ds(1, 1), :]] + [moved[d, pl.ds(1, 1), :] for d in hops]
    uneven = jnp.where(gx >= nx // 2, 1.0 * rim, 0.0)
    counts = []
    for d in range(nx):
        source = behind(d)
        sign = jnp.where(source == 0, 1.0, 0.0) - jnp.where(source == nx - 1, 1.0, 0.0)
        counts.append(rows + uneven * sign)
    mean_panel = sum(n * m for n, m in zip(counts, means)) / total
    spread = sum(squares) + sum(n * jnp.square(m - mean_panel) for n, m in zip(counts, means))
    factor = 1.0 / jnp.sqrt(spread / total + 1e-06)
    for copy in cross_copies:
        copy.wait_recv()
    value = score[...]
    for d in hops:
        value = value + arrived[d].astype(F32)
    score[...] = value * factor

    for copy in line_copies + twin_copies + raw_copies + back_copies + moment_copies + cross_copies:
        copy.wait_send()
    for copy in core_copies + pair_copies + to_pair + to_core + onward:
        copy.wait_send()

    @pl.when(gx < nx - 1)
    def _():
        for copy in up_copies:
            copy.wait_send()

    @pl.when(gx > 0)
    def _():
        for copy in down_copies:
            copy.wait_send()


def body(pressure, fir_taps, influence, mode_impulse, mode_taps):
    nx, ny, nz = (lax.axis_size(name) for name in ("gx", "gy", "gz"))
    rows, panels = pressure.shape
    total = rows * nx
    rim = fir_taps.shape[0] - 1
    modes = influence.shape[0]
    own = modes // (nx * ny * nz)
    own_panels = panels // nx
    dyn = mode_impulse.shape[1]
    fits = own % 16 == 0 and lax.axis_size("wind") == 2 and modes % 32 == 0 and ny == nz == 2 and rows % SPAN == 0 and own_panels % COLS == 0 and nx % 2 == 0
    if not fits or rim % LEAD or dyn > LEAD:
        return plain_body(pressure, fir_taps, influence, mode_impulse, mode_taps)

    first_mode = lax.axis_index(("gx", "gy", "gz")) * own
    own_impulse = lax.dynamic_slice_in_dim(mode_impulse, first_mode, own, 0)
    own_limits = lax.dynamic_slice_in_dim(mode_taps, first_mode, own, 0)
    kept = jnp.arange(dyn, dtype=jnp.int32)[None, :] < own_limits[:, None]
    gains = jnp.where(kept, own_impulse, 0.0)
    width = SPAN + rim
    tap_rows = jnp.broadcast_to(jnp.pad(fir_taps, (0, width - rim - 1))[None], (16, width))

    vmem = pl.BlockSpec(memory_space=pltpu.VMEM)
    responses, scores = pl.pallas_call(
        functools.partial(tower_kernel, nx, own, dyn),
        out_shape=(
            jax.ShapeDtypeStruct((own, total), BF16),
            jax.ShapeDtypeStruct((modes, own_panels), F32),
        ),
        in_specs=[vmem, pl.BlockSpec(memory_space=pl.ANY), vmem, vmem],
        out_specs=(vmem, vmem),
        scratch_shapes=[
            pltpu.VMEM((rows, panels), BF16),
            pltpu.SemaphoreType.DMA,
            pltpu.VMEM((nx, modes, own_panels), BF16),
            pltpu.VMEM((nx, 2, 2, own, rows), F32),
            pltpu.VMEM((nx, 2, own, rows), F32),
            pltpu.VMEM((nx, 2, own, rows), F32),
            pltpu.VMEM((nx, own, rows), F32),
            pltpu.VMEM((nx, own, rows), F32),
            pltpu.VMEM((nx, own, rows), F32),
            pltpu.VMEM((own, rim + total), F32),
            pltpu.VMEM((own, LEAD + total), F32),
            pltpu.VMEM((dyn, own, LEAD), F32),
            pltpu.VMEM((own, total + rim), BF16),
            pltpu.VMEM((SPAN, width), BF16),
            pltpu.VMEM((SPAN, width), BF16),
            pltpu.VMEM((rim, panels // 2), BF16),
            pltpu.VMEM((rim, panels // 2), BF16),
            pltpu.VMEM((rim, panels // 2), BF16),
            pltpu.VMEM((rows, panels), BF16),
            pltpu.VMEM((nx, own, rows), BF16),
            pltpu.VMEM((nx, 2, 2, own, rows), BF16),
            pltpu.VMEM((nx, modes, own_panels), BF16),
            pltpu.VMEM((nx, modes, own_panels), BF16),
            pltpu.VMEM((nx, 8, own_panels), F32),
            pltpu.VMEM((nx, 8, own_panels), F32),
            pltpu.SemaphoreType.DMA((11 * nx + 10,)),
            pltpu.SemaphoreType.DMA((11 * nx + 10,)),
        ],
        compiler_params=pltpu.CompilerParams(
            collective_id=0, has_side_effects=True, vmem_limit_bytes=48 * 1024 * 1024
        ),
    )(influence.reshape(modes, own_panels), pressure, tap_rows, gains)
    return responses, scores.reshape(influence.shape)


def solution(mesh):
    return jax.shard_map(
        body,
        mesh=mesh,
        in_specs=(
            P(("wind", "gx"), ("gy", "gz")),
            P(),
            P(None, ("gy", "gz"), "gx", None),
            P(),
            P(),
        ),
        out_specs=(P(("wind", "gx", "gy", "gz"), None), P("wind", ("gy", "gz"), "gx", None)),
        check_vma=False,
    )
```
